32 devices in a mesh: dp: 8 (over z, x), tensor: 4 (over y, core).
Axes of the slice: x: 2, y: 2, z: 4, core: 2. Of those that a mesh axis runs over, the one named last changes fastest.
Arguments:
- tokens: bfloat16 [8192, 1024], P('dp'), may hold values from -6 to 6
- positions: int32 [8192], P('dp'), may hold values from -1 to 1023, as said below
- attn_gain: bfloat16 [1024], P('dp'), may hold values from 0.5 to 1.5
- query_gain: bfloat16 [64], replicated, may hold values from 0.25 to 1.75
- key_gain: bfloat16 [64], replicated, may hold values from 0.25 to 1.75
- w_query: bfloat16 [1024, 1024], P('dp', 'tensor'), may hold values from -0.1875 to 0.1875
- w_key: bfloat16 [1024, 512], P('dp', 'tensor'), may hold values from -0.1875 to 0.1875
- w_value: bfloat16 [1024, 512], P('dp', 'tensor'), may hold values from -0.1875 to 0.1875
- w_out: bfloat16 [1024, 1024], P('tensor', 'dp'), may hold values from -2 to 2
- ffn_gain: bfloat16 [1024], P('dp'), may hold values from 0.5 to 1.5
- w_gate: bfloat16 [1024, 4608], P('dp', 'tensor'), may hold values from -0.1875 to 0.1875
- w_up: bfloat16 [1024, 4608], P('dp', 'tensor'), may hold values from -0.1875 to 0.1875
- w_down: bfloat16 [4608, 1024], P('tensor', 'dp'), may hold values from -0.09375 to 0.09375
- cotangent: bfloat16 [8192, 1024], P('dp'), may hold values from -6 to 6
Outputs:
- block_output: bfloat16 [8192, 1024], P(('dp', 'tensor'))
- input_grad: bfloat16 [8192, 1024], P(('dp', 'tensor'))
- grad_attn_gain: float32 [1024], P('dp')
- grad_query_gain: float32 [64], replicated
- grad_key_gain: float32 [64], replicated
- grad_w_query: float32 [1024, 1024], P('dp', 'tensor')
- grad_w_key: float32 [1024, 512], P('dp', 'tensor')
- grad_w_value: float32 [1024, 512], P('dp', 'tensor')
- grad_w_out: float32 [1024, 1024], P('tensor', 'dp')
- grad_ffn_gain: float32 [1024], P('dp')
- grad_w_gate: float32 [1024, 4608], P('dp', 'tensor')
- grad_w_up: float32 [1024, 4608], P('dp', 'tensor')
- grad_w_down: float32 [4608, 1024], P('tensor', 'dp')
The draws below stay inside these ranges and needn't reach their ends.
Inputs may be any that keep to these rules, and one draw needn't show every extreme that they name: Each group of 1024 slots of one index of dp holds whole sequences packed from its first slot: positions count 0, 1, 2, ... within a sequence, and slots after the last sequence hold -1. Every group fills at least half of its slots, and one group holds a single sequence of all 1024 slots.
All inputs are finite; a program needn't handle non-finite values.
Results may differ from the reference program's by a relative error of at most 0.018.
Values may be sent and summed in bfloat16 or wider, within the bound.
No kernel may reach another device: no remote copies, remote signals or barrier semaphores. Data moves between devices by JAX's collectives and lax.ppermute only.
A program may use at most 128 MiB of HBM per device.

```python
import jax
import jax.numpy as jnp
from jax import lax

D = 1024
HEADS = 16
KV = 8
HD = 64
FF = 4608
TOK_DEV = 1024
TOKENS = 8192
N_DP = 8


def draw_positions(key, part):
    key = jax.random.fold_in(key, 7)
    first_key, second_key, third_key = jax.random.split(key, 3)
    fills = jax.random.randint(first_key, (N_DP,), TOK_DEV // 2, TOK_DEV + 1)
    chosen = jax.random.randint(second_key, (), 0, N_DP)
    groups = jnp.arange(N_DP, dtype=jnp.int32)
    fills = jnp.where(groups == chosen, TOK_DEV, fills)
    slots = jnp.arange(TOK_DEV, dtype=jnp.int32)[None, :]
    starts = jax.random.randint(third_key, (N_DP, TOK_DEV), 0, max(TOK_DEV // 4, 2)) == 0
    starts = starts & (groups[:, None] != chosen)
    starts = starts | (slots == 0)
    latest = lax.cummax(jnp.where(starts, slots, 0), axis=1)
    placed = jnp.where(slots < fills[:, None], slots - latest, -1)
    return placed.reshape(N_DP * TOK_DEV).astype(jnp.int32)


def raised(values, stream_key, source, target, blocks, factor):
    owner, partner = [(jnp.arange(values.shape[position]) // (values.shape[position] // blocks)).reshape([-1 if axis == position else 1 for axis in range(values.ndim)]) for position in (source, target)]
    chosen = jax.random.permutation(stream_key, blocks)[partner]
    strong = (owner == chosen) | (owner == (partner + blocks // 2) % blocks)
    return jnp.where(strong, factor * values, values)


def level_of(rng, shape, pieces, smallest, top_value):
    loudness = 1.0
    for dim, shards_of in pieces:
        heights = jax.random.uniform(jax.random.fold_in(jax.random.fold_in(rng, 6), dim), (shards_of,), jnp.float32, smallest / len(pieces), top_value / len(pieces))
        loudness = loudness * jnp.repeat(jnp.exp(heights), shape[dim] // shards_of).reshape((-1,) + (1,) * (len(shape) - 1 - dim))
    return loudness


def normal_values(key, dims, scale, reach, shards=(), held_as=jnp.bfloat16):
    values = jax.random.normal(key, dims, jnp.float32) * scale
    if len(shards) > 0:
        values = level_of(key, dims, shards, -0.22, 0.18) * values
    return jnp.clip(values, min=-reach, max=reach).astype(held_as)


def bell_draw_with(rng, shape, width, most, pieces, heavy, kind=jnp.bfloat16):
    result = width * jax.random.normal(rng, shape, jnp.float32)
    if pieces:
        result = result * level_of(rng, shape, pieces, -0.22, 0.18)
    return jnp.clip(raised(result, jax.random.fold_in(rng, 3), *heavy), -most, most).astype(kind)


def setup_inputs(seed: int = 0) -> dict:
    streams_of = jax.random.split(jax.random.key(seed), 15)
    return {
        "tokens": normal_values(streams_of[0], (TOKENS, D), 1.0, 6.0, ((0, 8),)),
        "positions": draw_positions(jax.random.fold_in(streams_of[14], 71), 0),
        "attn_gain": jnp.clip(1.0 + 0.1 * jax.random.normal(streams_of[2], (D,), jnp.float32), 0.5, 1.5).astype(jnp.bfloat16),
        "query_gain": jnp.clip(1.0 + 0.15 * jax.random.normal(streams_of[3], (HD,), jnp.float32), 0.25, 1.75).astype(jnp.bfloat16),
        "key_gain": jnp.clip(1.0 + 0.15 * jax.random.normal(streams_of[4], (HD,), jnp.float32), 0.25, 1.75).astype(jnp.bfloat16),
        "w_query": normal_values(streams_of[5], (D, HEADS * HD), D ** -0.5, 0.1875, ((0, 8), (1, 4))),
        "w_key": normal_values(streams_of[6], (D, KV * HD), D ** -0.5, 0.1875, ((0, 8), (1, 4))),
        "w_value": normal_values(streams_of[7], (D, KV * HD), D ** -0.5, 0.1875, ((0, 8), (1, 4))),
        "w_out": normal_values(streams_of[8], (HEADS * HD, D), (HEADS * HD // 128) ** -0.5, 2.0, ((0, 4), (1, 8))),
        "ffn_gain": jnp.clip(1.0 + 0.1 * jax.random.normal(streams_of[9], (D,), jnp.float32), 0.5, 1.5).astype(jnp.bfloat16),
        "w_gate": normal_values(streams_of[10], (D, FF), D ** -0.5, 0.1875, ((0, 8), (1, 4))),
        "w_up": normal_values(streams_of[11], (D, FF), D ** -0.5, 0.1875, ((0, 8), (1, 4))),
        "w_down": normal_values(streams_of[12], (FF, D), FF ** -0.5, 0.09375, ((0, 4), (1, 8))),
        "cotangent": bell_draw_with(streams_of[13], (TOKENS, D), 1.0, 6.0, ((0, 8),), (0, 1, 8, 2.0)),
    }


@jax.custom_vjp
def low(v):
    return lax.optimization_barrier(v.astype(jnp.bfloat16)).astype(jnp.float32)

@jax.custom_vjp
def low_back(v):
    return v

def low_keep(v):
    return (low(v), None)

def low_pass(kept, grad):
    return (grad,)

def back_keep(v):
    return (v, None)

def back_low(kept, grad):
    return (low(grad),)
low.defvjp(low_keep, low_pass)
low_back.defvjp(back_keep, back_low)
epsilon = 1e-05
rope_base = 1000000.0
negative = -1e+30

def highest(left, right):
    return jnp.dot(left, right, precision=lax.Precision.HIGHEST)

def norm_rows(values, scale_gain):
    inverse = lax.rsqrt(lax.optimization_barrier(jnp.mean(values * values, axis=-1, keepdims=True)) + epsilon)
    return values * inverse * scale_gain

def rotary_tables(slot_positions):
    halfway = HD // 2
    powers = jnp.arange(halfway, dtype=jnp.float32) * (2.0 / HD)
    frequency = rope_base ** (-powers)
    angles = jnp.maximum(slot_positions, 0).astype(jnp.float32)[:, None] * frequency[None, :]
    cosine = jnp.cos(angles)
    sine_table = jnp.sin(angles)
    return (jnp.concatenate([cosine, cosine], axis=-1)[:, None, :], jnp.concatenate([sine_table, sine_table], axis=-1)[:, None, :])

def rotate(values, cosine, sine_table):
    halfway = values.shape[-1] // 2
    turned = jnp.concatenate([-values[..., halfway:], values[..., :halfway]], axis=-1)
    return values * cosine + turned * sine_table

def allowed_pairs(slot_positions, row_start, row_count):
    slot_count = slot_positions.shape[0]
    live_keys = slot_positions >= 0
    segment = jnp.cumsum((slot_positions == 0).astype(jnp.int32)).astype(jnp.int32)
    key_index = jnp.arange(slot_count, dtype=jnp.int32)
    query_index = row_start.astype(jnp.int32) + jnp.arange(row_count, dtype=jnp.int32)
    query_segment = lax.dynamic_slice_in_dim(segment, row_start.astype(jnp.int32), row_count)
    query_live = lax.dynamic_slice_in_dim(live_keys, row_start.astype(jnp.int32), row_count)
    same_segment = (query_segment[:, None] == segment[None, :]) & (key_index[None, :] <= query_index[:, None])
    same_segment = same_segment & query_live[:, None] & live_keys[None, :]
    return same_segment | (key_index[None, :] == query_index[:, None])

def attend(operands):
    query_block, key_block, value_block, slot_positions = operands
    slot_count = slot_positions.shape[0]
    allowed = allowed_pairs(slot_positions, jnp.int32(0), slot_count)
    scores = jnp.einsum('igrd,jgd->grij', query_block, key_block, precision=lax.Precision.HIGHEST) * HD ** (-0.5)
    scores = low_back(scores)
    scores = jnp.where(allowed, scores, negative)
    highest_score = lax.optimization_barrier(jnp.max(scores, axis=-1, keepdims=True))
    weights = jnp.where(allowed, jnp.exp(scores - highest_score), 0.0)
    shares = weights / lax.optimization_barrier(jnp.sum(weights, axis=-1, keepdims=True))
    return jnp.einsum('grij,jgd->igrd', low(shares), value_block, precision=lax.Precision.HIGHEST)

def reference(tokens, positions, attn_gain, query_gain, key_gain, w_query, w_key, w_value, w_out, ffn_gain, w_gate, w_up, w_down, cotangent):
    cosine, sine_table = rotary_tables(positions)
    grouped = HEADS // KV

    def forward(inputs, gain_attn, gain_query, gain_key, weight_query, weight_key, weight_value, weight_out, gain_ffn, weight_gate, weight_up, weight_down):
        normed = low(norm_rows(inputs, gain_attn))
        queries = low_back(highest(normed, weight_query)).reshape(TOKENS, HEADS, HD)
        keys_all = low_back(highest(normed, weight_key)).reshape(TOKENS, KV, HD)
        values_all = low_back(highest(normed, weight_value)).reshape(TOKENS, KV, HD)
        queries = low(rotate(norm_rows(queries, gain_query), cosine, sine_table))
        keys_all = low(rotate(norm_rows(keys_all, gain_key), cosine, sine_table))
        values_all = low(values_all)
        attended = lax.map(jax.checkpoint(attend), (queries.reshape(N_DP, TOK_DEV, KV, grouped, HD), keys_all.reshape(N_DP, TOK_DEV, KV, HD), values_all.reshape(N_DP, TOK_DEV, KV, HD), positions.reshape(N_DP, TOK_DEV)))
        attended = low(low_back(attended.reshape(TOKENS, HEADS * HD)))
        residual = inputs + low_back(highest(attended, weight_out))
        normed_ffn = low(norm_rows(residual, gain_ffn))
        gate_proj = low_back(highest(normed_ffn, weight_gate))
        up_proj = low_back(highest(normed_ffn, weight_up))
        hidden = low(jax.nn.silu(gate_proj) * up_proj)
        return residual + low_back(highest(hidden, weight_down))
    output, pullback = jax.vjp(forward, tokens.astype(jnp.float32), attn_gain.astype(jnp.float32), query_gain.astype(jnp.float32), key_gain.astype(jnp.float32), w_query.astype(jnp.float32), w_key.astype(jnp.float32), w_value.astype(jnp.float32), w_out.astype(jnp.float32), ffn_gain.astype(jnp.float32), w_gate.astype(jnp.float32), w_up.astype(jnp.float32), w_down.astype(jnp.float32))
    live_rows = (positions >= 0).astype(jnp.float32)[:, None]
    gradients = pullback(cotangent.astype(jnp.float32) * live_rows)
    return (output.astype(jnp.bfloat16), gradients[0].astype(jnp.bfloat16), gradients[1], gradients[2], gradients[3], gradients[4], gradients[5], gradients[6], gradients[7], gradients[8], gradients[9], gradients[10], gradients[11])
```

```python
import functools

import jax
import jax.numpy as jnp
import numpy as np
from jax import lax
from jax.experimental import pallas as pl
from jax.experimental.pallas import tpu as pltpu
from jax.sharding import PartitionSpec as P

HD = 64
LANES = 128
epsilon = 1e-05
rope_base = 1000000.0
score_scale = HD ** (-0.5)
bf16 = jnp.bfloat16
f32 = jnp.float32
whole_vmem = pl.BlockSpec(memory_space=pltpu.VMEM)
scalars = pl.BlockSpec(memory_space=pltpu.SMEM)


def product(left, right):
    return jnp.dot(left, right, preferred_element_type=f32)


def contract_rows(left, right):
    return lax.dot_general(left, right, (((0,), (0,)), ((), ())), preferred_element_type=f32)


def contract_cols(left, right):
    return lax.dot_general(left, right, (((1,), (1,)), ((), ())), preferred_element_type=f32)


def norm_parts(values, scale_gain):
    inverse = lax.rsqrt(jnp.mean(values * values, axis=-1, keepdims=True) + epsilon)
    normed = values * inverse
    return (normed * scale_gain, normed, inverse)


def norm_back(upstream, scale_gain, normed, inverse):
    scaled = upstream * scale_gain
    inner_sum = jnp.mean(scaled * normed, axis=-1, keepdims=True)
    return inverse * (scaled - normed * inner_sum)


def ring_order(count):
    return list(range(0, count, 2)) + list(range(count - 1, 0, -2))


def ring_pairs(count):
    order = ring_order(count)
    ahead = [(order[i], order[(i + 1) % count]) for i in range(count)]
    return ahead, [(b, a) for a, b in ahead]


def ring_gather(block, count):
    ahead, back = ring_pairs(count)
    blocks = [None] * count
    blocks[0] = block
    up = down = block
    for step in range(1, count // 2):
        up = lax.ppermute(up, "dp", ahead)
        down = lax.ppermute(down, "dp", back)
        blocks[count - step] = up
        blocks[step] = down
    cut = block.shape[0] // 2
    top = lax.ppermute(up[:cut], "dp", ahead)
    bottom = lax.ppermute(down[cut:], "dp", back)
    blocks[count // 2] = jnp.concatenate([top, bottom], axis=0)
    return blocks


def ring_scatter(blocks, count):
    ahead, back = ring_pairs(count)
    half = count // 2
    cut = blocks[0].shape[0] // 2
    up = lax.ppermute(blocks[half][:cut], "dp", ahead)
    down = lax.ppermute(blocks[half][cut:], "dp", back)
    for step in range(half - 1, 0, -1):
        mine_up, mine_down = blocks[step], blocks[count - step]
        if step == half - 1:
            next_up = jnp.concatenate([add(mine_up[:cut], up), mine_up[cut:]], axis=0)
            next_down = jnp.concatenate([mine_down[:cut], add(mine_down[cut:], down)], axis=0)
        else:
            next_up, next_down = add(mine_up, up), add(mine_down, down)
        up = lax.ppermute(next_up, "dp", ahead)
        down = lax.ppermute(next_down, "dp", back)
    return blocks[0].astype(f32) + up.astype(f32) + down.astype(f32)


def add(left, right):
    return (left.astype(f32) + right.astype(f32)).astype(bf16)


def swap(values, axis, bit):
    count = lax.axis_size(axis)
    return lax.ppermute(values, axis, [(i, i ^ bit) for i in range(count)])


def tensor_scatter(part):
    rows = part.shape[0] // 4
    block = [part[k * rows : (k + 1) * rows] for k in range(4)]
    other = swap(jnp.concatenate([block[1], block[3]], axis=0), "tensor", 1)
    far = swap(add(block[2], other[rows:]), "tensor", 2)
    return block[0].astype(f32) + other[:rows].astype(f32) + far.astype(f32)


def tensor_gather(rows_here):
    far = swap(rows_here, "tensor", 2)
    near = swap(jnp.concatenate([rows_here, far], axis=0), "tensor", 1)
    rows = rows_here.shape[0]
    return jnp.concatenate([rows_here, near[:rows], far, near[rows:]], axis=0)


def sum_all(values):
    for axis in ("tensor", "dp"):
        bit = 1
        while bit < lax.axis_size(axis):
            values = values + swap(values, axis, bit)
            bit *= 2
    return values


def arrange_kernel(row_map, col_map, source, out):
    for k in range(out.shape[1] // LANES):
        start = pl.multiple_of(col_map[k] * LANES, LANES)
        out[:, k * LANES : (k + 1) * LANES] = source[:, pl.ds(start, LANES)]


def arrange(values, row_map, col_map):
    rows, cols = values.shape
    count = row_map.shape[0]
    return pl.pallas_call(
        arrange_kernel,
        out_shape=jax.ShapeDtypeStruct((rows, cols), values.dtype),
        grid_spec=pltpu.PrefetchScalarGridSpec(
            num_scalar_prefetch=2,
            grid=(count,),
            in_specs=[pl.BlockSpec((rows // count, cols), lambda i, r, c: (r[i], 0))],
            out_specs=pl.BlockSpec((rows // count, cols), lambda i, r, c: (i, 0)),
        ),
        name="arrange",
    )(row_map, col_map, values)


def lane_ids(rows):
    return lax.broadcasted_iota(jnp.int32, (rows, LANES), 1)


def head_sums(values):
    row = lax.broadcasted_iota(jnp.int32, (LANES, LANES), 0) < HD
    col = lax.broadcasted_iota(jnp.int32, (LANES, LANES), 1) < HD
    ones = jnp.where(row == col, 1.0, 0.0).astype(bf16)
    high = values.astype(bf16)
    rest = (values - high.astype(f32)).astype(bf16)
    return product(high, ones) + product(rest, ones)


def turn(values, sign):
    first = (lane_ids(values.shape[0]) % HD) < HD // 2
    ahead = pltpu.roll(values, LANES - HD // 2, 1)
    behind = pltpu.roll(values, HD // 2, 1)
    return jnp.where(first, -sign * ahead, sign * behind)


def spread_heads(values, fill):
    low = lane_ids(values.shape[0]) < HD
    moved = pltpu.roll(values, HD, 1)
    return (
        jnp.where(low, values, fill),
        jnp.where(low, fill, moved),
        jnp.where(low, moved, fill),
        jnp.where(low, fill, values),
    )


def forward_kernel(
    place, qkv, cosine, sine, reach, gain_q, gain_k,
    attended, inverse_total, q_out, k_out, v_out, keys, values, total,
):
    blocks, size = 4, qkv.shape[0] // 4
    low = lane_ids(size) < HD

    def prepare(a, carry):
        here = pl.ds(pl.multiple_of(a * size, size), size)
        there = pl.ds(pl.multiple_of((a ^ place[0]) * size, size), size)
        cos_here, sin_here = cosine[here, :], sine[here, :]

        def turned(x, gain):
            inverse = lax.rsqrt(head_sums(x * x) * (1.0 / HD) + epsilon)
            y = x * inverse * gain
            return y * cos_here + turn(y, 1.0) * sin_here

        for g in range(2):
            q = turned(qkv[there, g * LANES : (g + 1) * LANES], gain_q[...])
            q_out[here, g * LANES : (g + 1) * LANES] = (q.astype(bf16).astype(f32) * score_scale).astype(bf16)
        k = turned(qkv[there, 2 * LANES : 3 * LANES], gain_k[...]).astype(bf16)
        v = qkv[there, 3 * LANES : 4 * LANES].astype(bf16)
        k_out[here, :] = k
        v_out[here, :] = v
        for h, (one, two) in enumerate(zip(spread_heads(k.astype(f32), 0.0), spread_heads(v.astype(f32), 1.0))):
            keys[h, here, :] = one.astype(bf16)
            values[h, here, :] = two.astype(bf16)
        return carry

    lax.fori_loop(0, blocks, prepare, 0)
    offset = lax.broadcasted_iota(jnp.int32, (size, size), 0) - lax.broadcasted_iota(jnp.int32, (size, size), 1)

    def query_block(i, carry):
        here = pl.ds(pl.multiple_of(i * size, size), size)
        there = pl.ds(pl.multiple_of((i ^ place[0]) * size, size), size)
        total[...] = jnp.zeros_like(total)
        reach_here = jnp.concatenate([reach[here, :]] * (size // LANES), axis=1)

        def key_block(j, inner):
            at = pl.ds(pl.multiple_of(j * size, size), size)
            distance = offset + (i - j) * size
            allowed = (distance >= 0) & (distance <= reach_here)
            for h in range(4):
                q = q_out[here, (h // 2) * LANES : (h // 2 + 1) * LANES]
                weights = jnp.where(allowed, jnp.exp(contract_cols(q, keys[h, at, :])), 0.0)
                total[h] += product(weights.astype(bf16), values[h, at, :])
            return inner

        lax.fori_loop(0, i + 1, key_block, 0)
        for g in range(2):
            first, second = total[2 * g], total[2 * g + 1]
            inverse = 1.0 / pltpu.roll(jnp.where(low, second, first), HD, 1)
            cols = slice(g * LANES, (g + 1) * LANES)
            attended[there, cols] = (jnp.where(low, first, second) * inverse).astype(bf16)
            inverse_total[here, cols] = inverse
        return carry

    lax.fori_loop(0, blocks, query_block, 0)


def backward_kernel(
    place, qkv, cosine, sine, reach, gain_q, gain_k, q_in, k_in, v_in, attended, inverse_total, grad_in,
    grad_qkv, grad_gain, keys, values, keys_t, grad_scaled, grad_aug, dq_t, dk, dk_sum, dv_sum,
):
    blocks, size = 4, qkv.shape[0] // 4
    lane = lane_ids(size)
    low = lane < HD

    def prepare(a, carry):
        here = pl.ds(pl.multiple_of(a * size, size), size)
        there = pl.ds(pl.multiple_of((a ^ place[0]) * size, size), size)
        k = k_in[here, :].astype(f32)
        v = v_in[here, :].astype(f32)
        for h, (one, two) in enumerate(zip(spread_heads(k, 0.0), spread_heads(v, 1.0))):
            keys[h, here, :] = one.astype(bf16)
            keys_t[h, a] = one.T.astype(bf16)
            values[h, here, :] = two.astype(bf16)
        for g in range(2):
            cols = slice(g * LANES, (g + 1) * LANES)
            upstream = grad_in[there, cols].astype(f32)
            inverse = inverse_total[here, cols]
            delta = head_sums(upstream * attended[there, cols].astype(f32)) * inverse
            scaled = upstream * inverse
            grad_scaled[here, cols] = scaled.astype(bf16)
            moved = -pltpu.roll(delta, HD, 1)
            high = moved.astype(bf16).astype(f32)
            rest = moved - high
            spare = jnp.where(lane % HD == 0, high, jnp.where(lane % HD == 1, rest, 0.0))
            grad_aug[2 * g, here, :] = jnp.where(low, scaled, spare).astype(bf16)
            grad_aug[2 * g + 1, here, :] = jnp.where(low, spare, scaled).astype(bf16)
            dq_t[g, a] = jnp.zeros((LANES, size), f32)
        return carry

    lax.fori_loop(0, blocks, prepare, 0)
    offset = lax.broadcasted_iota(jnp.int32, (size, size), 1) - lax.broadcasted_iota(jnp.int32, (size, size), 0)

    def key_block(j, carry):
        at = pl.ds(pl.multiple_of(j * size, size), size)
        dk_sum[...] = jnp.zeros_like(dk_sum)
        dv_sum[...] = jnp.zeros_like(dv_sum)

        def query_block(i, inner):
            here = pl.ds(pl.multiple_of(i * size, size), size)
            distance = offset + (i - j) * size
            allowed = (distance >= 0) & (distance <= reach[i])
            for g in range(2):
                cols = slice(g * LANES, (g + 1) * LANES)
                q = q_in[here, cols]
                upstream = grad_scaled[here, cols]
                dk_parts, dv_parts = [], []
                for h in (2 * g, 2 * g + 1):
                    weights = jnp.where(allowed, jnp.exp(contract_cols(keys[h, at, :], q)), 0.0)
                    share_grad = contract_cols(values[h, at, :], grad_aug[h, here, :])
                    score_grad = (weights * share_grad).astype(bf16)
                    dv_parts.append(product(weights.astype(bf16), upstream))
                    dk_parts.append(product(score_grad, q))
                    dq_t[g, i] += product(keys_t[h, j], score_grad)
                dk_sum[g] += jnp.where(low, dk_parts[0], dk_parts[1])
                dv_sum[g] += jnp.where(low, dv_parts[0], dv_parts[1])
            return inner

        lax.fori_loop(j, blocks, query_block, 0)
        there = pl.ds(pl.multiple_of((j ^ place[0]) * size, size), size)

        def folded(sums):
            both = [sums[g] + pltpu.roll(sums[g], HD, 1) for g in range(2)]
            return jnp.where(low, both[0], both[1])

        dk[at, :] = folded(dk_sum)
        grad_qkv[there, 3 * LANES : 4 * LANES] = folded(dv_sum).astype(bf16)
        return carry

    lax.fori_loop(0, blocks, key_block, 0)
    grad_gain[...] = jnp.zeros_like(grad_gain)

    def finish(a, carry):
        here = pl.ds(pl.multiple_of(a * size, size), size)
        there = pl.ds(pl.multiple_of((a ^ place[0]) * size, size), size)
        cos_here, sin_here = cosine[here, :], sine[here, :]
        for part in range(3):
            cols = slice(part * LANES, (part + 1) * LANES)
            gain = gain_q[...] if part < 2 else gain_k[...]
            upstream = dq_t[part, a].T * score_scale if part < 2 else dk[here, :]
            upstream = upstream * cos_here - turn(upstream * sin_here, 1.0)
            x = qkv[there, cols]
            inverse = lax.rsqrt(head_sums(x * x) * (1.0 / HD) + epsilon)
            normed = x * inverse
            scaled = upstream * gain
            inner_sum = head_sums(scaled * normed) * (1.0 / HD)
            grad_qkv[there, cols] = (inverse * (scaled - normed * inner_sum)).astype(bf16)
            grad_gain[0:1, cols] += jnp.sum(upstream * normed, axis=0, keepdims=True)
        return carry

    lax.fori_loop(0, blocks, finish, 0)


def attention_forward(place, qkv, cosine, sine, reach, gain_q, gain_k):
    slots = qkv.shape[0]
    return pl.pallas_call(
        forward_kernel,
        out_shape=(
            jax.ShapeDtypeStruct((slots, 2 * LANES), bf16),
            jax.ShapeDtypeStruct((slots, 2 * LANES), f32),
            jax.ShapeDtypeStruct((slots, 2 * LANES), bf16),
            jax.ShapeDtypeStruct((slots, LANES), bf16),
            jax.ShapeDtypeStruct((slots, LANES), bf16),
        ),
        in_specs=[scalars] + [whole_vmem] * 6,
        out_specs=(whole_vmem,) * 5,
        scratch_shapes=[
            pltpu.VMEM((4, slots, LANES), bf16),
            pltpu.VMEM((4, slots, LANES), bf16),
            pltpu.VMEM((4, slots // 4, LANES), f32),
        ],
        compiler_params=pltpu.CompilerParams(vmem_limit_bytes=32 * 2**20),
        cost_estimate=pl.CostEstimate(flops=6 * 10**9, bytes_accessed=6 * 2**20, transcendentals=3 * 10**6),
        name="attention_forward",
    )(place, qkv, cosine, sine, reach, gain_q, gain_k)


def attention_backward(place, qkv, cosine, sine, reach, gain_q, gain_k, saved, attended, upstream):
    slots = qkv.shape[0]
    size = slots // 4
    inverse_total, q, k, v = saved
    return pl.pallas_call(
        backward_kernel,
        out_shape=(
            jax.ShapeDtypeStruct((slots, 4 * LANES), bf16),
            jax.ShapeDtypeStruct((8, 3 * LANES), f32),
        ),
        in_specs=[scalars] + [whole_vmem] * 12,
        out_specs=(whole_vmem,) * 2,
        scratch_shapes=[
            pltpu.VMEM((4, slots, LANES), bf16),
            pltpu.VMEM((4, slots, LANES), bf16),
            pltpu.VMEM((4, 4, LANES, size), bf16),
            pltpu.VMEM((slots, 2 * LANES), bf16),
            pltpu.VMEM((4, slots, LANES), bf16),
            pltpu.VMEM((2, 4, LANES, size), f32),
            pltpu.VMEM((slots, LANES), f32),
            pltpu.VMEM((2, size, LANES), f32),
            pltpu.VMEM((2, size, LANES), f32),
        ],
        compiler_params=pltpu.CompilerParams(vmem_limit_bytes=32 * 2**20),
        cost_estimate=pl.CostEstimate(flops=15 * 10**9, bytes_accessed=8 * 2**20, transcendentals=3 * 10**6),
        name="attention_backward",
    )(place, qkv, cosine, sine, reach, gain_q, gain_k, q, k, v, attended, inverse_total, upstream)


def rotary_tables(slot_positions):
    powers = jnp.arange(HD // 2, dtype=f32) * (2.0 / HD)
    frequency = rope_base ** (-powers)
    angles = jnp.maximum(slot_positions, 0).astype(f32)[:, None] * frequency[None, :]
    return jnp.tile(jnp.cos(angles), (1, 4)), jnp.tile(jnp.sin(angles), (1, 4))


def per_device(
    tokens, positions, attn_gain, query_gain, key_gain, w_query, w_key, w_value, w_out, ffn_gain,
    w_gate, w_up, w_down, cotangent,
):
    slots, width = tokens.shape
    count = lax.axis_size("dp")
    me = lax.axis_index("dp")
    place = lax.axis_index("tensor").astype(jnp.int32)
    rows = slots // 4
    ring = count * LANES == width and count % 2 == 0
    hidden = w_gate.shape[1]

    groups = width // LANES
    if ring:
        order = np.array(ring_order(count), np.int32)
        where_is = np.argsort(order).astype(np.int32)
        spot = jnp.asarray(where_is)[me]
        col_map = jnp.asarray(order)[(spot + jnp.arange(count, dtype=jnp.int32)) % count]
        col_back = (jnp.asarray(where_is) - spot + count) % count
    else:
        col_map = col_back = jnp.arange(groups, dtype=jnp.int32)
    row_map = jnp.arange(4, dtype=jnp.int32) ^ place
    one_row = jnp.zeros((1,), jnp.int32)

    def gather(block, axis):
        if ring:
            return ring_gather(block, count)
        return lax.all_gather(block, "dp", axis=axis, tiled=True)

    qkv_shard = jnp.concatenate([w_query, w_key, w_value], axis=1)
    gains_shard = jnp.concatenate([attn_gain, ffn_gain])
    gate_up_shard = jnp.concatenate([w_gate, w_up], axis=1)
    if ring:
        pad = jnp.zeros((16, qkv_shard.shape[1]), bf16).at[0, : 2 * LANES].set(gains_shard)
        first = ring_gather(jnp.concatenate([qkv_shard, pad], axis=0), count)
        full_qkv = jnp.concatenate([b[:LANES] for b in first], axis=0)
        gain_attn = jnp.concatenate([b[LANES, :LANES] for b in first])
        gain_ffn = jnp.concatenate([b[LANES, LANES : 2 * LANES] for b in first])
        full_out = jnp.concatenate(ring_gather(w_out, count), axis=1)
        full_gate_up = jnp.concatenate(ring_gather(gate_up_shard, count), axis=0)
        full_down = jnp.concatenate(ring_gather(w_down, count), axis=1)
    else:
        full_qkv = lax.all_gather(qkv_shard, "dp", axis=0, tiled=True)
        gain_attn = lax.all_gather(attn_gain, "dp", axis=0, tiled=True)
        gain_ffn = lax.all_gather(ffn_gain, "dp", axis=0, tiled=True)
        full_out = lax.all_gather(w_out, "dp", axis=1, tiled=True)
        full_gate_up = lax.all_gather(gate_up_shard, "dp", axis=0, tiled=True)
        full_down = lax.all_gather(w_down, "dp", axis=1, tiled=True)
    gain_attn = gain_attn.astype(f32)
    gain_ffn = gain_ffn.astype(f32)

    def scatter(grad, axis):
        if ring:
            step = grad.shape[axis] // count
            parts = [lax.slice_in_dim(grad, k * step, (k + 1) * step, axis=axis) for k in range(count)]
            return ring_scatter(parts, count)
        return lax.psum_scatter(grad, "dp", scatter_dimension=axis, tiled=True).astype(f32)

    live = (positions >= 0).astype(bf16)[:, None]
    inputs = arrange(tokens, row_map, col_map)
    output_low = arrange(cotangent * live, row_map, col_map)
    cosine, sine = rotary_tables(positions)
    reach = jnp.maximum(positions, 0)
    reach_cols = jnp.broadcast_to(reach[:, None], (slots, LANES))
    reach_rows = reach.reshape(4, 1, rows)
    gain_q = jnp.tile(query_gain.astype(f32), 2)[None, :]
    gain_k = jnp.tile(key_gain.astype(f32), 2)[None, :]
    spot_row = place[None]

    attn_scaled, attn_normed, attn_inverse = norm_parts(inputs.astype(f32), gain_attn)
    normed_low = attn_scaled.astype(bf16)
    qkv = product(normed_low, full_qkv)
    attended, *saved = attention_forward(spot_row, qkv, cosine, sine, reach_cols, gain_q, gain_k)
    attn_rows = tensor_scatter(product(attended, full_out).astype(bf16))
    residual = inputs[:rows].astype(f32) + attn_rows
    ffn_scaled, ffn_normed, ffn_inverse = norm_parts(residual, gain_ffn)
    ffn_low = tensor_gather(ffn_scaled.astype(bf16))
    gate_up = product(ffn_low, full_gate_up)
    gate, up = gate_up[:, :hidden], gate_up[:, hidden:]
    gate_sigmoid = jax.nn.sigmoid(gate)
    gate_silu = gate * gate_sigmoid
    hidden_low = (gate_silu * up).astype(bf16)
    output_rows = residual + tensor_scatter(product(hidden_low, full_down).astype(bf16))
    block_output = arrange(output_rows.astype(bf16), one_row, col_back)

    grad_down = contract_rows(hidden_low, output_low).astype(bf16)
    hidden_grad = contract_cols(output_low, full_down)
    gate_grad = (hidden_grad * up * (gate_sigmoid * (1.0 + gate * (1.0 - gate_sigmoid)))).astype(bf16)
    up_grad = (hidden_grad * gate_silu).astype(bf16)
    gate_up_grad = jnp.concatenate([gate_grad, up_grad], axis=1)
    ffn_in_part = contract_cols(gate_up_grad, full_gate_up)
    ffn_in_rows = tensor_scatter(ffn_in_part.astype(bf16))
    grad_gate_up = contract_rows(ffn_low, gate_up_grad).astype(bf16)
    residual_grad = output_low[:rows].astype(f32) + norm_back(ffn_in_rows, gain_ffn, ffn_normed, ffn_inverse)
    ffn_gain_part = jnp.sum(ffn_in_rows * ffn_normed, axis=0)
    residual_low = tensor_gather(residual_grad.astype(bf16))
    grad_out = contract_rows(attended, residual_low).astype(bf16)
    attended_grad = contract_cols(residual_low, full_out).astype(bf16)
    grad_qkv_rows, gain_sums = attention_backward(
        spot_row, qkv, cosine, sine, reach_rows, gain_q, gain_k, saved, attended, attended_grad
    )
    grad_qkv = contract_rows(normed_low, grad_qkv_rows).astype(bf16)
    attn_in_part = contract_cols(grad_qkv_rows, full_qkv)
    attn_gain_part = jnp.sum(attn_in_part * attn_normed, axis=0)
    attn_in_rows = tensor_scatter(attn_in_part.astype(bf16))
    input_rows = residual_grad + norm_back(attn_in_rows, gain_attn, attn_normed[:rows], attn_inverse[:rows])
    input_grad = arrange(input_rows.astype(bf16), one_row, col_back)

    gain_vector = jnp.concatenate(
        [
            jnp.take(attn_gain_part.reshape(groups, LANES), col_back, axis=0).reshape(-1),
            jnp.take(ffn_gain_part.reshape(groups, LANES), col_back, axis=0).reshape(-1),
            gain_sums[0],
        ]
    )
    gain_total = sum_all(gain_vector)
    share = width // count
    grad_attn_gain = lax.dynamic_slice_in_dim(gain_total, me * share, share)
    grad_ffn_gain = lax.dynamic_slice_in_dim(gain_total, width + me * share, share)
    heads = gain_total[2 * width :].reshape(-1, HD)
    grad_query_gain = jnp.sum(heads[:4], axis=0)
    grad_key_gain = jnp.sum(heads[4:], axis=0)

    shard_qkv = scatter(grad_qkv, 0)
    shard_gate_up = scatter(grad_gate_up, 0)
    shard_out = scatter(grad_out, 1)
    shard_down = scatter(grad_down, 1)
    q_cols, k_cols = w_query.shape[1], w_key.shape[1]
    return (
        block_output,
        input_grad,
        grad_attn_gain,
        grad_query_gain,
        grad_key_gain,
        shard_qkv[:, :q_cols],
        shard_qkv[:, q_cols : q_cols + k_cols],
        shard_qkv[:, q_cols + k_cols :],
        shard_out,
        grad_ffn_gain,
        shard_gate_up[:, :hidden],
        shard_gate_up[:, hidden:],
        shard_down,
    )


def solution(mesh):
    in_specs = (
        P("dp", None), P("dp"), P("dp"), P(), P(), P("dp", "tensor"), P("dp", "tensor"), P("dp", "tensor"),
        P("tensor", "dp"), P("dp"), P("dp", "tensor"), P("dp", "tensor"), P("tensor", "dp"), P("dp", None),
    )
    out_specs = (
        P(("dp", "tensor"), None), P(("dp", "tensor"), None), P("dp"), P(), P(), P("dp", "tensor"),
        P("dp", "tensor"), P("dp", "tensor"), P("tensor", "dp"), P("dp"), P("dp", "tensor"), P("dp", "tensor"),
        P("tensor", "dp"),
    )
    return jax.shard_map(
        per_device, mesh=mesh, in_specs=in_specs, out_specs=out_specs, check_vma=False
    )
```

```python
import functools

import jax
import jax.numpy as jnp
import numpy as np
from jax import lax
from jax.experimental import pallas as pl
from jax.experimental.pallas import tpu as pltpu
from jax.sharding import PartitionSpec as P

HD = 64
LANES = 128
epsilon = 1e-05
rope_base = 1000000.0
score_scale = HD ** (-0.5)
bf16 = jnp.bfloat16
f32 = jnp.float32
whole_vmem = pl.BlockSpec(memory_space=pltpu.VMEM)
scalars = pl.BlockSpec(memory_space=pltpu.SMEM)


def product(left, right):
    return jnp.dot(left, right, preferred_element_type=f32)


def contract_rows(left, right):
    return lax.dot_general(left, right, (((0,), (0,)), ((), ())), preferred_element_type=f32)


def contract_cols(left, right):
    return lax.dot_general(left, right, (((1,), (1,)), ((), ())), preferred_element_type=f32)


def ring_order(count):
    return list(range(0, count, 2)) + list(range(count - 1, 0, -2))


def ring_pairs(count):
    order = ring_order(count)
    ahead = [(order[i], order[(i + 1) % count]) for i in range(count)]
    return ahead, [(b, a) for a, b in ahead]


def tied(first, others):
    flat = lax.optimization_barrier((*first, *others))
    return flat[: len(first)], flat[len(first) :]


def after(values, needed):
    return tied(values, needed)[0]


class RingGather:
    def __init__(self, block, count):
        self.count, self.step = count, 0
        self.blocks = [block] + [None] * (count - 1)
        self.moving = (block, block)

    def send(self):
        ahead, back = ring_pairs(self.count)
        up, down = self.moving
        self.step += 1
        if self.step == self.count // 2:
            up, down = up[:HD], down[HD:]
        self.moving = (lax.ppermute(up, "dp", ahead), lax.ppermute(down, "dp", back))
        self.keep()

    def keep(self):
        half = self.count // 2
        if self.step < half:
            self.blocks[self.count - self.step], self.blocks[self.step] = self.moving
        else:
            self.blocks[half] = self.moving

    def tie(self, *others):
        self.moving, others = tied(self.moving, others)
        self.keep()
        return others

    def pieces(self):
        half = self.count // 2
        return [*self.blocks[:half], *self.blocks[half], *self.blocks[half + 1 :]]


class RingScatter:
    def __init__(self, blocks, top, bottom, count):
        self.blocks, self.count, self.step = blocks, count, count // 2
        self.moving = (top, bottom)

    def send(self):
        ahead, back = ring_pairs(self.count)
        self.moving = (lax.ppermute(self.moving[0], "dp", ahead), lax.ppermute(self.moving[1], "dp", back))
        self.step -= 1

    def add(self):
        up, down = self.moving
        mine_up, mine_down = self.blocks(self.step), self.blocks(self.count - self.step)
        if self.step == self.count // 2 - 1:
            up = jnp.concatenate([add(mine_up[:HD], up), mine_up[HD:]], axis=0)
            down = jnp.concatenate([mine_down[:HD], add(mine_down[HD:], down)], axis=0)
        else:
            up, down = add(mine_up, up), add(mine_down, down)
        self.moving = (up, down)

    def tie(self, *others):
        self.moving, others = tied(self.moving, others)
        return others


def pieces_of(full):
    blocks = [full[k * LANES : (k + 1) * LANES] for k in range(full.shape[0] // LANES)]
    half = len(blocks) // 2
    return blocks[:half] + [blocks[half][:HD], blocks[half][HD:]] + blocks[half + 1 :]


def add(left, right):
    return (left.astype(f32) + right.astype(f32)).astype(bf16)


def swap(values, axis, bit):
    count = lax.axis_size(axis)
    return lax.ppermute(values, axis, [(i, i ^ bit) for i in range(count)])


def tensor_scatter(send, keep):
    rows = send.shape[0] // 2
    other = swap(send, "tensor", 1)
    far = swap(add(keep[rows:], other[rows:]), "tensor", 2)
    return other, far


def tensor_gather(mine):
    near = swap(mine, "tensor", 1)
    far = swap(mine, "tensor", 2)
    return near, swap(far, "tensor", 1), mine, far


def sum_all(values):
    for axis in ("tensor", "dp"):
        bit = 1
        while bit < lax.axis_size(axis):
            values = values + swap(values, axis, bit)
            bit *= 2
    return values


def column(place, k, count):
    if not count:
        return k * LANES
    spot = place[1] + k
    spot = jnp.where(spot >= count, spot - count, spot)
    return pl.multiple_of(jnp.where(spot < count // 2, 2 * spot, 2 * count - 1 - 2 * spot) * LANES, LANES)


def lane_ids(rows):
    return lax.broadcasted_iota(jnp.int32, (rows, LANES), 1)


def head_sums(values):
    row = lax.broadcasted_iota(jnp.int32, (LANES, LANES), 0) < HD
    col = lax.broadcasted_iota(jnp.int32, (LANES, LANES), 1) < HD
    ones = jnp.where(row == col, 1.0, 0.0).astype(bf16)
    high = values.astype(bf16)
    rest = (values - high.astype(f32)).astype(bf16)
    return product(high, ones) + product(rest, ones)


def turn(values, sign):
    first = (lane_ids(values.shape[0]) % HD) < HD // 2
    ahead = pltpu.roll(values, LANES - HD // 2, 1)
    behind = pltpu.roll(values, HD // 2, 1)
    return jnp.where(first, -sign * ahead, sign * behind)


def spread_heads(values, fill):
    low = lane_ids(values.shape[0]) < HD
    moved = pltpu.roll(values, HD, 1)
    return (
        jnp.where(low, values, fill),
        jnp.where(low, fill, moved),
        jnp.where(low, moved, fill),
        jnp.where(low, fill, values),
    )


def assemble(pieces, out):
    row = 0
    for k, piece in enumerate(pieces):
        count = HD if k in (4, 5) else LANES
        out[row : row + count, :] = piece[:count, :]
        row += count


def row_norm(values):
    inverse = lax.rsqrt(jnp.mean(values * values, axis=-1, keepdims=True) + epsilon)
    return values * inverse, inverse


def project_kernel(
    place, tokens, cos_part, sin_part, gain_q, gain_k, p0, p1, p2, p3, p4, p5, p6, p7, p8,
    weights_out, gains, normed_low, qkv, q_out, k_out, v_out, cosine, sine,
):
    blocks, size = 4, qkv.shape[0] // 4
    pieces = (p0, p1, p2, p3, p4, p5, p6, p7, p8)
    assemble(pieces, weights_out)
    column = 0
    for k, piece in enumerate(pieces):
        if k == 4:
            continue
        at = HD if k == 5 else LANES
        row = piece[at : at + 16, :].astype(f32)
        gains[0:1, column : column + LANES] = row[0:1, :LANES]
        gains[1:2, column : column + LANES] = row[0:1, LANES : 2 * LANES]
        column += LANES

    def project(a, carry):
        here = pl.ds(pl.multiple_of(a * size, size), size)
        normed, _ = row_norm(tokens[here, :].astype(f32))
        h = (normed * gains[0:1, :]).astype(bf16)
        normed_low[here, :] = h
        qkv[here, :] = product(h, weights_out[:, : 4 * LANES])
        return carry

    lax.fori_loop(0, blocks, project, 0)

    def prepare(a, carry):
        here = pl.ds(pl.multiple_of(a * size, size), size)
        there = pl.ds(pl.multiple_of((a ^ place[0]) * size, size), size)
        cos_here = jnp.concatenate([cos_part[here, :]] * 4, axis=1)
        sin_here = jnp.concatenate([sin_part[here, :]] * 4, axis=1)
        cosine[here, :], sine[here, :] = cos_here, sin_here

        def turned(x, gain):
            inverse = lax.rsqrt(head_sums(x * x) * (1.0 / HD) + epsilon)
            y = x * inverse * gain
            return y * cos_here + turn(y, 1.0) * sin_here

        for g in range(2):
            q = turned(qkv[there, g * LANES : (g + 1) * LANES], gain_q[...])
            q_out[here, g * LANES : (g + 1) * LANES] = (q.astype(bf16).astype(f32) * score_scale).astype(bf16)
        k = turned(qkv[there, 2 * LANES : 3 * LANES], gain_k[...]).astype(bf16)
        v = qkv[there, 3 * LANES : 4 * LANES].astype(bf16)
        k_out[here, :] = k
        v_out[here, :] = v
        return carry

    lax.fori_loop(0, blocks, prepare, 0)


def attention_kernel(
    place, places, weights, q_in, k_in, v_in, attended, inverse_total, send, keep, keys, values, total,
):
    blocks, size = 4, q_in.shape[0] // 4
    low = lane_ids(size) < HD

    def prepare(a, carry):
        here = pl.ds(pl.multiple_of(a * size, size), size)
        k, v = k_in[here, :].astype(f32), v_in[here, :].astype(f32)
        for h, (one, two) in enumerate(zip(spread_heads(k, 0.0), spread_heads(v, 1.0))):
            keys[h, here, :] = one.astype(bf16)
            values[h, here, :] = two.astype(bf16)
        return carry

    lax.fori_loop(0, blocks, prepare, 0)
    offset = lax.broadcasted_iota(jnp.int32, (size, size), 0) - lax.broadcasted_iota(jnp.int32, (size, size), 1)

    def query_block(i, carry):
        here = pl.ds(pl.multiple_of(i * size, size), size)
        there = pl.ds(pl.multiple_of((i ^ place[0]) * size, size), size)
        total[...] = jnp.zeros_like(total)
        reach_here = jnp.concatenate([jnp.maximum(places[here, :], 0)] * (size // LANES), axis=1)

        def key_block(j, inner):
            at = pl.ds(pl.multiple_of(j * size, size), size)
            distance = offset + (i - j) * size
            allowed = (distance >= 0) & (distance <= reach_here)
            for h in range(4):
                q = q_in[here, (h // 2) * LANES : (h // 2 + 1) * LANES]
                weights = jnp.where(allowed, jnp.exp(contract_cols(q, keys[h, at, :])), 0.0)
                total[h] += product(weights.astype(bf16), values[h, at, :])
            return inner

        lax.fori_loop(0, i + 1, key_block, 0)
        for g in range(2):
            first, second = total[2 * g], total[2 * g + 1]
            inverse = 1.0 / pltpu.roll(jnp.where(low, second, first), HD, 1)
            cols = slice(g * LANES, (g + 1) * LANES)
            attended[there, cols] = (jnp.where(low, first, second) * inverse).astype(bf16)
            inverse_total[here, cols] = inverse
        return carry

    lax.fori_loop(0, blocks, query_block, 0)
    for j, (out, half) in enumerate([(keep, 0), (send, 0), (keep, 1), (send, 1)]):
        rows = slice(j * size, (j + 1) * size)
        out[half * size : (half + 1) * size, :] = contract_cols(attended[rows, :], weights[:, 4 * LANES :]).astype(bf16)


def backward_kernel(
    place, places, weights, q_in, k_in, v_in, attended, inverse_total, near, near_far, mine, far,
    dq_out, dk_out, dv_out, grad_in, keys, values, keys_t, grad_scaled, grad_aug, dq_t, dk_sum, dv_sum,
):
    blocks, size = 4, q_in.shape[0] // 4
    lane = lane_ids(size)
    low = lane < HD
    for j, rows in enumerate((mine, near, far, near_far)):
        grad_in[j * size : (j + 1) * size, :] = product(rows[...], weights[:, 4 * LANES :]).astype(bf16)

    def prepare(a, carry):
        here = pl.ds(pl.multiple_of(a * size, size), size)
        there = pl.ds(pl.multiple_of((a ^ place[0]) * size, size), size)
        k = spread_heads(k_in[here, :].astype(f32), 0.0)
        v = spread_heads(v_in[here, :].astype(f32), 1.0)
        for h in range(4):
            keys[h, here, :] = k[h].astype(bf16)
            keys_t[h, a] = k[h].T.astype(bf16)
            values[h, here, :] = v[h].astype(bf16)
        for g in range(2):
            cols = slice(g * LANES, (g + 1) * LANES)
            upstream = grad_in[there, cols].astype(f32)
            inverse = inverse_total[here, cols]
            delta = head_sums(upstream * attended[there, cols].astype(f32)) * inverse
            scaled = upstream * inverse
            grad_scaled[here, cols] = scaled.astype(bf16)
            moved = -pltpu.roll(delta, HD, 1)
            high = moved.astype(bf16).astype(f32)
            spare = jnp.where(lane % HD == 0, high, jnp.where(lane % HD == 1, moved - high, 0.0))
            grad_aug[2 * g, here, :] = jnp.where(low, scaled, spare).astype(bf16)
            grad_aug[2 * g + 1, here, :] = jnp.where(low, spare, scaled).astype(bf16)
            dq_t[g, a] = jnp.zeros((LANES, size), f32)
        return carry

    lax.fori_loop(0, blocks, prepare, 0)
    offset = lax.broadcasted_iota(jnp.int32, (size, size), 1) - lax.broadcasted_iota(jnp.int32, (size, size), 0)

    def key_block(j, carry):
        at = pl.ds(pl.multiple_of(j * size, size), size)
        dk_sum[...] = jnp.zeros_like(dk_sum)
        dv_sum[...] = jnp.zeros_like(dv_sum)

        def query_block(i, inner):
            here = pl.ds(pl.multiple_of(i * size, size), size)
            distance = offset + (i - j) * size
            allowed = (distance >= 0) & (distance <= jnp.maximum(places[i], 0))
            for g in range(2):
                cols = slice(g * LANES, (g + 1) * LANES)
                q = q_in[here, cols]
                upstream = grad_scaled[here, cols]
                dk_parts, dv_parts, dq_parts = [], [], []
                for h in (2 * g, 2 * g + 1):
                    weights_t = jnp.where(allowed, jnp.exp(contract_cols(keys[h, at, :], q)), 0.0)
                    share_grad = contract_cols(values[h, at, :], grad_aug[h, here, :])
                    score_grad = (weights_t * share_grad).astype(bf16)
                    dv_parts.append(product(weights_t.astype(bf16), upstream))
                    dk_parts.append(product(score_grad, q))
                    dq_parts.append(product(keys_t[h, j], score_grad))
                dq_t[g, i] += dq_parts[0] + dq_parts[1]
                dk_sum[g] += jnp.where(low, dk_parts[0], dk_parts[1])
                dv_sum[g] += jnp.where(low, dv_parts[0], dv_parts[1])
            return inner

        lax.fori_loop(j, blocks, query_block, 0)

        def folded(sums):
            both = [sums[g] + pltpu.roll(sums[g], HD, 1) for g in range(2)]
            return jnp.where(low, both[0], both[1])

        dk_out[at, :] = folded(dk_sum)
        dv_out[at, :] = folded(dv_sum).astype(bf16)
        return carry

    lax.fori_loop(0, blocks, key_block, 0)

    def finish(a, carry):
        here = pl.ds(pl.multiple_of(a * size, size), size)
        for g in range(2):
            dq_out[here, g * LANES : (g + 1) * LANES] = dq_t[g, a].T * score_scale
        return carry

    lax.fori_loop(0, blocks, finish, 0)


def backward_end_kernel(
    ring, place, tokens, weights, normed_low, qkv, cosine, sine, gain_q, gain_k, attended,
    near, near_far, mine, far, ffn_gain, dq, dk, dv,
    grad_weights, top, bottom, send, keep, grad_attn, grad_gain, grad_qkv,
):
    blocks, size = 4, qkv.shape[0] // 4
    grad_gain[...] = jnp.zeros_like(grad_gain)

    def finish(a, carry):
        here = pl.ds(pl.multiple_of(a * size, size), size)
        there = pl.ds(pl.multiple_of((a ^ place[0]) * size, size), size)
        cos_here, sin_here = cosine[here, :], sine[here, :]
        for part in range(3):
            cols = slice(part * LANES, (part + 1) * LANES)
            gain = gain_q[...] if part < 2 else gain_k[...]
            upstream = dq[here, cols] if part < 2 else dk[here, :]
            upstream = upstream * cos_here - turn(upstream * sin_here, 1.0)
            x = qkv[there, cols]
            inverse = lax.rsqrt(head_sums(x * x) * (1.0 / HD) + epsilon)
            normed = x * inverse
            scaled = upstream * gain
            inner_sum = head_sums(scaled * normed) * (1.0 / HD)
            grad_qkv[there, cols] = (inverse * (scaled - normed * inner_sum)).astype(bf16)
            grad_gain[0:1, cols] += jnp.sum(upstream * normed, axis=0, keepdims=True)
        grad_qkv[there, 3 * LANES : 4 * LANES] = dv[here, :]
        return carry

    lax.fori_loop(0, blocks, finish, 0)
    grad_attn[...] = jnp.zeros_like(grad_attn)
    for j, (out, half) in enumerate([(keep, 0), (send, 0), (keep, 1), (send, 1)]):
        here = slice(j * size, (j + 1) * size)
        back = contract_cols(grad_qkv[here, :], weights[:, : 4 * LANES])
        out[half * size : (half + 1) * size, :] = back.astype(bf16)
        normed, _ = row_norm(tokens[here, :].astype(f32))
        grad_attn[...] += jnp.sum(back * normed, axis=0, keepdims=True)
    blocks = tokens.shape[1] // LANES
    extra = grad_weights.shape[0] // blocks - LANES
    for k in range(0, blocks, 2):
        cols = slice(k * LANES, (k + 2) * LANES)
        first = contract_rows(normed_low[:, cols], grad_qkv[...]).astype(bf16)
        second = jnp.zeros((2 * LANES, 2 * LANES), f32)
        for j, rows in enumerate((mine, near, far, near_far)):
            second += contract_rows(rows[:, cols], attended[j * size : (j + 1) * size, :])
        for n in range(2):
            at = (k + n) * (LANES + extra)
            rows = slice(n * LANES, (n + 1) * LANES)
            grad_weights[at : at + LANES, : 4 * LANES] = first[rows]
            grad_weights[at : at + LANES, 4 * LANES :] = second[rows].astype(bf16)
    if not ring:
        top[...] = jnp.zeros_like(top)
        bottom[...] = jnp.zeros_like(bottom)
        return
    heads = [grad_gain[0:1, part * LANES : (part + 1) * LANES] for part in range(3)]
    heads = [jnp.broadcast_to(h, (8, LANES)) for h in (heads[0] + heads[1], heads[2])]
    heads = [h + pltpu.roll(h, HD, 1) for h in heads]
    heads = jnp.where(lane_ids(8) < HD, heads[0], heads[1])[0:1]
    for k in range(blocks):
        cols = slice(k * LANES, (k + 1) * LANES)
        at = k * (LANES + extra) + LANES
        row = lax.broadcasted_iota(jnp.int32, (extra, LANES), 0) == 0
        for n, values in enumerate((grad_attn[:, cols], ffn_gain[:, cols], heads)):
            values = jnp.where(row, jnp.broadcast_to(values, (extra, LANES)), 0.0)
            grad_weights[at : at + extra, n * LANES : (n + 1) * LANES] = values.astype(bf16)
        grad_weights[at : at + extra, 3 * LANES :] = jnp.zeros((extra, 3 * LANES), bf16)
    half = blocks // 2 * (LANES + extra)
    top[...] = grad_weights[half : half + HD, :]
    bottom[...] = grad_weights[half + HD : half + LANES + extra, :]


def pack_kernel(w_query, w_key, w_value, w_out, gains, out):
    wide = w_query.shape[1]
    out[:LANES, :wide] = w_query[...]
    out[:LANES, wide : wide + LANES] = w_key[...]
    out[:LANES, wide + LANES : wide + 2 * LANES] = w_value[...]
    out[:LANES, wide + 2 * LANES :] = w_out[...].astype(f32).T.astype(bf16)
    out[LANES:, :] = gains[...]


def pack_ffn_kernel(w_gate, w_up, w_down, out):
    step = out.shape[1] // 3
    out[:, :step] = w_gate[...]
    out[:, step : 2 * step] = w_up[...]
    out[:, 2 * step :] = w_down[...].astype(f32).T.astype(bf16)


def unpack_ffn_kernel(mine, up, down, gate, up_out, down_out):
    step = gate.shape[1]

    def total(part):
        cols = slice(part * step, (part + 1) * step)
        return mine[:, cols].astype(f32) + up[:, cols].astype(f32) + down[:, cols].astype(f32)

    gate[...] = total(0)
    up_out[...] = total(1)
    down_out[...] = total(2).T


def unpack_kernel(mine, up, down, query, key, value, out, gains):
    wide = query.shape[1]
    total = mine[:LANES, :].astype(f32) + up[:LANES, :].astype(f32) + down[:LANES, :].astype(f32)
    rest = slice(LANES, LANES + 16)
    gains[...] = (mine[rest, :].astype(f32) + up[rest, :].astype(f32) + down[rest, :].astype(f32))[:8, : 3 * LANES]
    query[...] = total[:, :wide]
    key[...] = total[:, wide : wide + LANES]
    value[...] = total[:, wide + LANES : wide + 2 * LANES]
    out[...] = total[:, wide + 2 * LANES :].T


def arrange_kernel(ring, place, tokens, out):
    for k in range(tokens.shape[1] // LANES):
        out[:, k * LANES : (k + 1) * LANES] = tokens[:, pl.ds(column(place, k, ring), LANES)]


def arrange_live_kernel(ring, place, cotangent, places, out):
    live = places[...] >= 0
    for k in range(cotangent.shape[1] // LANES):
        values = cotangent[:, pl.ds(column(place, k, ring), LANES)].astype(f32)
        out[:, k * LANES : (k + 1) * LANES] = jnp.where(live, values, 0.0).astype(bf16)


def residual_kernel(part, other, far, tokens, gains, residual, low):
    total = part[...].astype(f32) + other[...].astype(f32) + far[...].astype(f32)
    total = tokens[...].astype(f32) + total
    residual[...] = total
    normed, _ = row_norm(total)
    low[...] = (normed * gains[1:2, :]).astype(bf16)


def put_columns(ring, place, out, values):
    for k in range(values.shape[1] // LANES):
        out[:, pl.ds(column(place, k, ring), LANES)] = values[:, k * LANES : (k + 1) * LANES].astype(out.dtype)


def norm_back(upstream, gain, normed, inverse):
    scaled = upstream * gain
    inner_sum = jnp.mean(scaled * normed, axis=-1, keepdims=True)
    return inverse * (scaled - normed * inner_sum)


def residual_back_kernel(part, other, far, residual, gains, output_low, grad, low, gain_out):
    upstream = part[...].astype(f32) + other[...].astype(f32) + far[...].astype(f32)
    normed, inverse = row_norm(residual[...])
    total = output_low[...].astype(f32) + norm_back(upstream, gains[1:2, :], normed, inverse)
    grad[...] = total
    low[...] = total.astype(bf16)
    gain_out[...] = jnp.sum(upstream * normed, axis=0, keepdims=True)


def output_kernel(ring, place, part, other, far, residual, out):
    total = part[...].astype(f32) + other[...].astype(f32) + far[...].astype(f32)
    put_columns(ring, place, out, residual[...] + total)


def input_back_kernel(ring, place, part, other, far, tokens, gains, grad, out):
    upstream = part[...].astype(f32) + other[...].astype(f32) + far[...].astype(f32)
    normed, inverse = row_norm(tokens[...].astype(f32))
    put_columns(ring, place, out, grad[...] + norm_back(upstream, gains[0:1, :], normed, inverse))


def ffn_kernel(near, near_far, mine, far, output_low, *refs):
    pieces, rest = refs[:9], refs[9:]
    low, active, out_send, out_keep, in_send, in_keep, weights = rest
    size = mine.shape[0]
    step = weights.shape[1] // 3
    half = pl.program_id(0)

    @pl.when(half == 0)
    def _():
        assemble(pieces, weights)
        low[:size, :] = near[...]
        low[size:, :] = near_far[...]

    @pl.when(half == 1)
    def _():
        low[:size, :] = mine[...]
        low[size:, :] = far[...]

    both = product(low[...], weights[:, : 2 * step])
    hidden_grad = product(output_low[...], weights[:, 2 * step :])
    gate, up = both[:, :step], both[:, step:]
    sigmoid = 1.0 / (1.0 + jnp.exp(-gate))
    silu = gate * sigmoid
    active[:, 2 * step :] = (silu * up).astype(bf16)
    active[:, :step] = (hidden_grad * up * (sigmoid + silu * (1.0 - sigmoid))).astype(bf16)
    active[:, step : 2 * step] = (hidden_grad * silu).astype(bf16)
    out = contract_cols(active[:, 2 * step :], weights[:, 2 * step :])
    into = contract_cols(active[:, : 2 * step], weights[:, : 2 * step])

    @pl.when(half == 0)
    def _():
        out_send[...] = out.astype(bf16)
        in_send[...] = into.astype(bf16)

    @pl.when(half == 1)
    def _():
        out_keep[...] = out.astype(bf16)
        in_keep[...] = into.astype(bf16)


def ffn_weights_kernel(low, output_low, active, out, top, bottom):
    step = active.shape[1] // 3
    out[:, : 2 * step] = product(low[...].T, active[:, : 2 * step]).astype(bf16)
    out[:, 2 * step :] = product(output_low[...].T, active[:, 2 * step :]).astype(bf16)

    @pl.when(pl.program_id(0) == 0)
    def _():
        top[...] = out[:HD, :]
        bottom[...] = out[HD:LANES, :]


def shape_of(*dims, dtype=bf16):
    return jax.ShapeDtypeStruct(dims, dtype)


def params(mebibytes=48):
    return pltpu.CompilerParams(vmem_limit_bytes=mebibytes * 2**20)


def cost(flops, bytes_moved, exps=0):
    return pl.CostEstimate(flops=int(flops), bytes_accessed=int(bytes_moved), transcendentals=int(exps))


def simple(kernel, outs, name, args, n_scalars=0):
    return pl.pallas_call(
        kernel,
        out_shape=outs,
        in_specs=[scalars] * n_scalars + [whole_vmem] * (len(args) - n_scalars),
        out_specs=jax.tree.map(lambda _: whole_vmem, outs),
        compiler_params=params(),
        name=name,
    )(*args)


def first_rows(rows, cols, at=0):
    return pl.BlockSpec((rows, cols), lambda i: (at, 0))


def own_rows(kernel, rows, width, outs, name, place, args, places=()):
    specs = [scalars] if place is not None else []
    specs += [first_rows(min(rows, a.shape[0]), width, dict(places).get(n, 0)) for n, a in enumerate(args)]
    return pl.pallas_call(
        kernel,
        grid=(1,),
        out_shape=outs,
        in_specs=specs,
        out_specs=tuple(first_rows(o.shape[0], width) for o in outs),
        compiler_params=params(),
        cost_estimate=cost(8 * rows * width, 12 * rows * width),
        name=name,
    )(*([place] if place is not None else []), *args)


def feed_forward(rows_in, output_low, pieces):
    slots, width = output_low.shape
    cols = pieces[0].shape[1]
    half = slots // 2
    wide = shape_of(half, width)
    moving = lambda n: pl.BlockSpec((half, n), lambda i: (i, 0))
    return pl.pallas_call(
        ffn_kernel,
        grid=(2,),
        out_shape=(shape_of(slots, width), shape_of(slots, cols), wide, wide, wide, wide),
        in_specs=[whole_vmem] * 4 + [moving(width)] + [whole_vmem] * 9,
        out_specs=(moving(width), moving(cols)) + (whole_vmem,) * 4,
        scratch_shapes=[pltpu.VMEM((width, cols), bf16)],
        compiler_params=params(56),
        cost_estimate=cost(4 * slots * width * cols, 20 * 2**20, 2e6),
        name="ffn",
    )(*rows_in, output_low, *pieces)


def feed_forward_weights(low, output_low, active, first, number):
    slots, width = low.shape
    cols = active.shape[1]
    pair = 2 * LANES
    pairs = width // pair
    side = pl.BlockSpec((slots, pair), lambda i: (0, lax.rem(i + first, pairs)))
    return pl.pallas_call(
        ffn_weights_kernel,
        grid=(number,),
        out_shape=(shape_of(number * pair, cols), shape_of(HD, cols), shape_of(HD, cols)),
        in_specs=[side, side, whole_vmem],
        out_specs=(pl.BlockSpec((pair, cols), lambda i: (i, 0)), whole_vmem, whole_vmem),
        compiler_params=params(),
        cost_estimate=cost(2 * slots * pair * number * cols, 12 * 2**20),
        name="ffn_weights",
    )(low, output_low, active)


def rotary_tables(slot_positions):
    powers = jnp.arange(HD // 2, dtype=f32) * (2.0 / HD)
    frequency = rope_base ** (-powers)
    angles = jnp.maximum(slot_positions, 0).astype(f32)[:, None] * frequency[None, :]
    return jnp.cos(angles), jnp.sin(angles)


def per_device(
    tokens, positions, attn_gain, query_gain, key_gain, w_query, w_key, w_value, w_out, ffn_gain,
    w_gate, w_up, w_down, cotangent,
):
    slots, width = tokens.shape
    count = lax.axis_size("dp")
    me = lax.axis_index("dp")
    place = lax.axis_index("tensor").astype(jnp.int32)
    rows = slots // 4
    ring = count * LANES == width and count % 2 == 0
    hidden = w_gate.shape[1]
    q_cols, k_cols = w_query.shape[1], w_key.shape[1]
    attn_cols = q_cols + 2 * k_cols + w_out.shape[0]

    if ring:
        spot = jnp.where(me % 2 == 0, me // 2, count - 1 - me // 2)
    else:
        spot = me
    length = count if ring else 0
    place = jnp.stack([place, spot.astype(jnp.int32)])

    def in_place(kernel):
        return functools.partial(kernel, length)

    if ring:
        gains_row = jnp.pad(
            jnp.concatenate([attn_gain, ffn_gain])[None, :], ((0, 15), (0, attn_cols - 2 * LANES))
        )
        attn_block = simple(
            pack_kernel, shape_of(LANES + 16, attn_cols), "pack", (w_query, w_key, w_value, w_out, gains_row)
        )
        ffn_block = simple(pack_ffn_kernel, shape_of(LANES, 3 * hidden), "pack_ffn", (w_gate, w_up, w_down))
    else:
        gathered = lax.all_gather(
            jnp.concatenate([w_query, w_key, w_value, w_out.T], axis=1), "dp", axis=0, tiled=True
        )
        gains_all = jnp.stack(
            [lax.all_gather(g, "dp", axis=0, tiled=True) for g in (attn_gain, ffn_gain)], axis=0
        )
        attn_pieces = []
        for k, piece in enumerate(pieces_of(gathered)):
            column = k * LANES if k < 4 else (k - 1) * LANES
            pad = jnp.pad(
                gains_all[:, column : column + LANES].reshape(1, -1), ((0, 15), (0, attn_cols - 2 * LANES))
            )
            attn_pieces.append(piece if k == 4 else jnp.concatenate([piece, pad], axis=0))
        turned = w_down.T
        block = jnp.concatenate([w_gate, w_up, turned], axis=1)
        ffn_pieces = pieces_of(lax.all_gather(block, "dp", axis=0, tiled=True))

    places = jnp.broadcast_to(positions[:, None], (slots, LANES))
    place_rows = positions.reshape(4, 1, rows)
    straight = pl.BlockSpec((rows, width), lambda i, s: (i, 0))

    def arranged(kernel, row_of, args, name):
        return pl.pallas_call(
            in_place(kernel),
            out_shape=shape_of(slots, width),
            grid_spec=pltpu.PrefetchScalarGridSpec(
                num_scalar_prefetch=1,
                grid=(4,),
                in_specs=[pl.BlockSpec((rows, a.shape[1]), lambda i, s: (row_of(i) ^ s[0], 0)) for a in args],
                out_specs=straight,
            ),
            cost_estimate=cost(0, 4 * slots * width),
            name=name,
        )(place, *args)

    inputs = arranged(arrange_kernel, lambda i: i, (tokens,), "arrange")
    output_low = arranged(arrange_live_kernel, lambda i: lax.rem(2 * i + 1, 5), (cotangent, places), "arrange_live")
    tables = rotary_tables(positions)
    if ring:
        attn_ring, ffn_ring = RingGather(attn_block, count), RingGather(ffn_block, count)
        attn_ring.send()
        attn_ring.tie(*ffn_ring.moving)
        attn_ring.send()
        (inputs,) = attn_ring.tie(inputs)
        attn_ring.send()
        tables = attn_ring.tie(*tables)
        attn_ring.send()
        ffn_ring.moving = after(ffn_ring.moving, attn_ring.moving)
        ffn_ring.send()
        attn_pieces = attn_ring.pieces()
    gain_q = jnp.tile(query_gain.astype(f32), 2)[None, :]
    gain_k = jnp.tile(key_gain.astype(f32), 2)[None, :]

    weights, gains, normed_low, qkv, q, k, v, cosine, sine = pl.pallas_call(
        project_kernel,
        out_shape=(
            shape_of(width, attn_cols),
            shape_of(8, width, dtype=f32),
            shape_of(slots, width),
            shape_of(slots, 4 * LANES, dtype=f32),
            shape_of(slots, 2 * LANES),
            shape_of(slots, LANES),
            shape_of(slots, LANES),
            shape_of(slots, LANES, dtype=f32),
            shape_of(slots, LANES, dtype=f32),
        ),
        in_specs=[scalars] + [whole_vmem] * 14,
        out_specs=(whole_vmem,) * 9,
        compiler_params=params(),
        cost_estimate=cost(3e9, 14 * 2**20, 3e6),
        name="project",
    )(place, inputs, *tables, gain_q, gain_k, *attn_pieces)
    halved = shape_of(slots // 2, width)
    attended, inverse_total, attn_send, attn_keep = pl.pallas_call(
        attention_kernel,
        out_shape=(shape_of(slots, 2 * LANES), shape_of(slots, 2 * LANES, dtype=f32), halved, halved),
        in_specs=[scalars] + [whole_vmem] * 5,
        out_specs=(whole_vmem,) * 4,
        scratch_shapes=[
            pltpu.VMEM((4, slots, LANES), bf16),
            pltpu.VMEM((4, slots, LANES), bf16),
            pltpu.VMEM((4, rows, LANES), f32),
        ],
        compiler_params=params(),
        cost_estimate=cost(9e9, 8 * 2**20, 3e6),
        name="attention",
    )(place, places, weights, q, k, v)

    other = swap(attn_send, "tensor", 1)
    if ring:
        (other,) = after((other,), ffn_ring.moving)
        ffn_ring.send()
    far = swap(add(attn_keep[rows:], other[rows:]), "tensor", 2)
    if ring:
        (far,) = after((far,), ffn_ring.moving)
        ffn_ring.send()
    row_f32, row_bf16 = shape_of(rows, width, dtype=f32), shape_of(rows, width)
    one_gain = shape_of(1, width, dtype=f32)
    residual, ffn_rows = own_rows(
        residual_kernel, rows, width, (row_f32, row_bf16), "residual", None, (attn_keep, other, far, inputs, gains)
    )
    near, far = swap(ffn_rows, "tensor", 1), swap(ffn_rows, "tensor", 2)
    if ring:
        (far,) = after((far,), ffn_ring.moving)
        ffn_ring.send()
        ffn_pieces = ffn_ring.pieces()
    rows_in = near, swap(far, "tensor", 1), ffn_rows, far

    ffn_low, active, out_send, out_keep, in_send, in_keep = feed_forward(rows_in, output_low, ffn_pieces)
    other = swap(in_send, "tensor", 1)
    if ring:
        half = count // 2
        toward_y = add(in_keep[rows:], other[rows:])
        (active,) = after((active,), (toward_y,))
        first_grad, top, bottom = feed_forward_weights(ffn_low, output_low, active, half // 2, 1)
        next_grad, _, _ = feed_forward_weights(ffn_low, output_low, active, half // 2 - 1, 1)
        ffn_grads = {half // 2: first_grad, half // 2 - 1: next_grad}

        def ffn_block_of(k):
            return ffn_grads[k // 2][k % 2 * LANES : (k % 2 + 1) * LANES]

        ffn_scatter = RingScatter(ffn_block_of, top, bottom, count)
        ffn_scatter.send()
        far = swap(toward_y, "tensor", 2)
    else:
        grad_ffn, _, _ = feed_forward_weights(ffn_low, output_low, active, 0, width // (2 * LANES))
        far = swap(add(in_keep[rows:], other[rows:]), "tensor", 2)
    residual_grad, residual_low, ffn_gain_part = own_rows(
        residual_back_kernel, rows, width, (row_f32, row_bf16, one_gain), "residual_back", None,
        (in_keep, other, far, residual, gains, output_low), [(5, 2)],
    )
    rows_back = tensor_gather(residual_low)
    if ring:
        (active,) = after((active,), (residual_low,))
        ffn_scatter.moving = after(ffn_scatter.moving, (residual_low,))
        ffn_scatter.add()
        ffn_scatter.send()
        rest_grad, _, _ = feed_forward_weights(ffn_low, output_low, active, half // 2 + 1, half // 2)
        ffn_grads[half // 2 + 1], ffn_grads[0] = rest_grad[: 2 * LANES], rest_grad[2 * LANES :]
        ffn_scatter.add()
        rows_back = after(rows_back, ffn_scatter.moving)
        ffn_scatter.send()

    grads = pl.pallas_call(
        backward_kernel,
        out_shape=(
            shape_of(slots, 2 * LANES, dtype=f32), shape_of(slots, LANES, dtype=f32), shape_of(slots, LANES),
        ),
        in_specs=[scalars] + [whole_vmem] * 11,
        out_specs=(whole_vmem,) * 3,
        scratch_shapes=[
            pltpu.VMEM((slots, 2 * LANES), bf16),
            pltpu.VMEM((4, slots, LANES), bf16),
            pltpu.VMEM((4, slots, LANES), bf16),
            pltpu.VMEM((4, 4, LANES, rows), bf16),
            pltpu.VMEM((slots, 2 * LANES), bf16),
            pltpu.VMEM((4, slots, LANES), bf16),
            pltpu.VMEM((2, 4, LANES, rows), f32),
            pltpu.VMEM((2, rows, LANES), f32),
            pltpu.VMEM((2, rows, LANES), f32),
        ],
        compiler_params=params(),
        cost_estimate=cost(16e9, 8 * 2**20, 3e6),
        name="attention_backward",
    )(place, place_rows, weights, q, k, v, attended, inverse_total, *rows_back)
    if ring:
        ffn_scatter.add()
        grads = after(grads, ffn_scatter.moving)
        ffn_scatter.send()
    tall = LANES + 16 if ring else LANES
    grad_attn, top, bottom, attn_send, attn_keep, attn_gain_part, head_gains = pl.pallas_call(
        in_place(backward_end_kernel),
        out_shape=(
            shape_of(width // LANES * tall, attn_cols),
            shape_of(HD, attn_cols),
            shape_of(tall - HD, attn_cols),
            halved,
            halved,
            one_gain,
            shape_of(8, 3 * LANES, dtype=f32),
        ),
        in_specs=[scalars] + [whole_vmem] * 17,
        out_specs=(whole_vmem,) * 7,
        scratch_shapes=[pltpu.VMEM((slots, 4 * LANES), bf16)],
        compiler_params=params(),
        cost_estimate=cost(9e9, 14 * 2**20),
        name="backward_end",
    )(
        place, inputs, weights, normed_low, qkv, cosine, sine, gain_q, gain_k, attended, *rows_back,
        ffn_gain_part, *grads,
    )

    (out_send,) = after((out_send,), rows_back)
    out_other, out_far = tensor_scatter(out_send, out_keep)
    (block_output,) = own_rows(
        in_place(output_kernel), rows, width, (row_bf16,), "output", place, (out_keep, out_other, out_far, residual)
    )
    other, far = tensor_scatter(attn_send, attn_keep)
    (input_grad,) = own_rows(
        in_place(input_back_kernel), rows, width, (row_bf16,), "input_back", place,
        (attn_keep, other, far, inputs, gains, residual_grad),
    )
    if ring:
        attn_scatter = RingScatter(lambda k: grad_attn[k * tall : (k + 1) * tall], top, bottom, count)
        attn_scatter.send()
        for step in range(half - 1):
            attn_scatter.add()
            if step == 0:
                attn_scatter.moving = after(attn_scatter.moving, ffn_scatter.moving)
            if step == half - 2:
                attn_scatter.moving = after(attn_scatter.moving, (far,))
            attn_scatter.send()
        shard_query, shard_key, shard_value, shard_out, gain_part = simple(
            unpack_kernel,
            (*(shape_of(*w.shape, dtype=f32) for w in (w_query, w_key, w_value, w_out)), shape_of(8, 3 * LANES, dtype=f32)),
            "unpack",
            (grad_attn[:tall], *attn_scatter.moving),
        )
        gain_total = gain_part + sum(swap(gain_part, "tensor", bits) for bits in (1, 2, 3))
        grad_attn_gain, grad_ffn_gain, heads = (gain_total[0, k * LANES : (k + 1) * LANES] for k in range(3))
        grad_query_gain, grad_key_gain = heads[:HD], heads[HD:]
        shard_gate, shard_up, shard_down = simple(
            unpack_ffn_kernel,
            tuple(jax.ShapeDtypeStruct(w.shape, f32) for w in (w_gate, w_up, w_down)),
            "unpack_ffn",
            (ffn_block_of(0), *ffn_scatter.moving),
        )
    else:
        gain_total = sum_all(jnp.concatenate([attn_gain_part, ffn_gain_part, head_gains[0:1]], axis=1))[0]
        share = width // count
        grad_attn_gain = lax.dynamic_slice_in_dim(gain_total, me * share, share)
        grad_ffn_gain = lax.dynamic_slice_in_dim(gain_total, width + me * share, share)
        heads = gain_total[2 * width :].reshape(-1, HD)
        grad_query_gain = jnp.sum(heads[:4], axis=0)
        grad_key_gain = jnp.sum(heads[4:], axis=0)
        total = lax.psum_scatter(grad_attn, "dp", scatter_dimension=0, tiled=True).astype(f32)
        shard_query, shard_key, shard_value, turned = jnp.split(total, np.cumsum([q_cols, k_cols, k_cols]), axis=1)
        shard_out = turned.T
        total = lax.psum_scatter(grad_ffn, "dp", scatter_dimension=0, tiled=True).astype(f32)
        shard_gate, shard_up, turned = jnp.split(total, 3, axis=1)
        shard_down = turned.T
    return (
        block_output,
        input_grad,
        grad_attn_gain,
        grad_query_gain,
        grad_key_gain,
        shard_query,
        shard_key,
        shard_value,
        shard_out,
        grad_ffn_gain,
        shard_gate,
        shard_up,
        shard_down,
    )


def solution(mesh):
    in_specs = (
        P("dp", None), P("dp"), P("dp"), P(), P(), P("dp", "tensor"), P("dp", "tensor"), P("dp", "tensor"),
        P("tensor", "dp"), P("dp"), P("dp", "tensor"), P("dp", "tensor"), P("tensor", "dp"), P("dp", None),
    )
    out_specs = (
        P(("dp", "tensor"), None), P(("dp", "tensor"), None), P("dp"), P(), P(), P("dp", "tensor"),
        P("dp", "tensor"), P("dp", "tensor"), P("tensor", "dp"), P("dp"), P("dp", "tensor"), P("dp", "tensor"),
        P("tensor", "dp"),
    )
    return jax.shard_map(
        per_device, mesh=mesh, in_specs=in_specs, out_specs=out_specs, check_vma=False
    )
```

```python
import functools

import jax
import jax.numpy as jnp
import numpy as np
from jax import lax
from jax.experimental import pallas as pl
from jax.experimental.pallas import tpu as pltpu
from jax.sharding import PartitionSpec as P

HD = 64
LANES = 128
epsilon = 1e-05
rope_base = 1000000.0
score_scale = HD ** (-0.5)
bf16 = jnp.bfloat16
f32 = jnp.float32
whole_vmem = pl.BlockSpec(memory_space=pltpu.VMEM)
scalars = pl.BlockSpec(memory_space=pltpu.SMEM)


def product(left, right):
    return jnp.dot(left, right, preferred_element_type=f32)


def contract_rows(left, right):
    return lax.dot_general(left, right, (((0,), (0,)), ((), ())), preferred_element_type=f32)


def contract_cols(left, right):
    return lax.dot_general(left, right, (((1,), (1,)), ((), ())), preferred_element_type=f32)


def ring_order(count):
    return list(range(0, count, 2)) + list(range(count - 1, 0, -2))


def ring_pairs(count):
    order = ring_order(count)
    ahead = [(order[i], order[(i + 1) % count]) for i in range(count)]
    return ahead, [(b, a) for a, b in ahead]


def tied(first, others):
    flat = lax.optimization_barrier((*first, *others))
    return flat[: len(first)], flat[len(first) :]


def after(values, needed):
    return tied(values, needed)[0]


class RingGather:
    def __init__(self, block, count):
        self.count, self.step = count, 0
        self.blocks = [block] + [None] * (count - 1)
        self.moving = (block, block)

    def send(self):
        ahead, back = ring_pairs(self.count)
        up, down = self.moving
        self.step += 1
        if self.step == self.count // 2:
            up, down = up[:HD], down[HD:]
        self.moving = (lax.ppermute(up, "dp", ahead), lax.ppermute(down, "dp", back))
        self.keep()

    def keep(self):
        half = self.count // 2
        if self.step < half:
            self.blocks[self.count - self.step], self.blocks[self.step] = self.moving
        else:
            self.blocks[half] = self.moving

    def tie(self, *others):
        self.moving, others = tied(self.moving, others)
        self.keep()
        return others

    def pieces(self):
        half = self.count // 2
        return [*self.blocks[:half], *self.blocks[half], *self.blocks[half + 1 :]]


class RingScatter:
    def __init__(self, blocks, top, bottom, count):
        self.blocks, self.count, self.step = blocks, count, count // 2
        self.moving = (top, bottom)

    def send(self):
        ahead, back = ring_pairs(self.count)
        self.moving = (lax.ppermute(self.moving[0], "dp", ahead), lax.ppermute(self.moving[1], "dp", back))
        self.step -= 1

    def add(self):
        up, down = self.moving
        mine_up, mine_down = self.blocks(self.step), self.blocks(self.count - self.step)
        if self.step == self.count // 2 - 1:
            up = add(mine_up, jnp.pad(up, ((0, mine_up.shape[0] - HD), (0, 0))))
            down = add(mine_down, jnp.pad(down, ((HD, 0), (0, 0))))
        else:
            up, down = add(mine_up, up), add(mine_down, down)
        self.moving = (up, down)

    def tie(self, *others):
        self.moving, others = tied(self.moving, others)
        return others


def pieces_of(full):
    blocks = [full[k * LANES : (k + 1) * LANES] for k in range(full.shape[0] // LANES)]
    half = len(blocks) // 2
    return blocks[:half] + [blocks[half][:HD], blocks[half][HD:]] + blocks[half + 1 :]


def add(left, right):
    return (left.astype(f32) + right.astype(f32)).astype(bf16)


def swap(values, axis, bit):
    count = lax.axis_size(axis)
    return lax.ppermute(values, axis, [(i, i ^ bit) for i in range(count)])


def tensor_scatter(send, keep):
    rows = send.shape[0] // 2
    other = swap(send, "tensor", 1)
    far = swap(add(keep[rows:], other[rows:]), "tensor", 2)
    return other, far


def tensor_gather(mine):
    near = swap(mine, "tensor", 1)
    far = swap(mine, "tensor", 2)
    return near, swap(far, "tensor", 1), mine, far


def sum_all(values):
    for axis in ("tensor", "dp"):
        bit = 1
        while bit < lax.axis_size(axis):
            values = values + swap(values, axis, bit)
            bit *= 2
    return values


def column(place, k, count):
    if not count:
        return k * LANES
    spot = place[1] + k
    spot = jnp.where(spot >= count, spot - count, spot)
    return pl.multiple_of(jnp.where(spot < count // 2, 2 * spot, 2 * count - 1 - 2 * spot) * LANES, LANES)


def lane_ids(rows):
    return lax.broadcasted_iota(jnp.int32, (rows, LANES), 1)


def head_sums(values):
    row = lax.broadcasted_iota(jnp.int32, (LANES, LANES), 0) < HD
    col = lax.broadcasted_iota(jnp.int32, (LANES, LANES), 1) < HD
    ones = jnp.where(row == col, 1.0, 0.0).astype(bf16)
    high = values.astype(bf16)
    rest = (values - high.astype(f32)).astype(bf16)
    return product(high, ones) + product(rest, ones)


def turn(values, sign):
    first = (lane_ids(values.shape[0]) % HD) < HD // 2
    ahead = pltpu.roll(values, LANES - HD // 2, 1)
    behind = pltpu.roll(values, HD // 2, 1)
    return jnp.where(first, -sign * ahead, sign * behind)


def spread_heads(values, fill):
    low = lane_ids(values.shape[0]) < HD
    moved = pltpu.roll(values, HD, 1)
    return (
        jnp.where(low, values, fill),
        jnp.where(low, fill, moved),
        jnp.where(low, moved, fill),
        jnp.where(low, fill, values),
    )


def assemble(pieces, out):
    row = 0
    for k, piece in enumerate(pieces):
        count = HD if k in (4, 5) else LANES
        out[row : row + count, :] = piece[:count, :]
        row += count


def row_norm(values):
    inverse = lax.rsqrt(jnp.mean(values * values, axis=-1, keepdims=True) + epsilon)
    return values * inverse, inverse


def project_kernel(
    place, tokens, cos_part, sin_part, gain_q, gain_k, p0, p1, p2, p3, p4, p5, p6, p7, p8,
    weights_out, gains, normed_low, qkv, q_out, k_out, v_out, cosine, sine,
):
    blocks, size = 4, qkv.shape[0] // 4
    pieces = (p0, p1, p2, p3, p4, p5, p6, p7, p8)
    assemble(pieces, weights_out)
    column = 0
    for k, piece in enumerate(pieces):
        if k == 4:
            continue
        at = HD if k == 5 else LANES
        row = piece[at : at + 16, :].astype(f32)
        gains[0:1, column : column + LANES] = row[0:1, :LANES]
        gains[1:2, column : column + LANES] = row[0:1, LANES : 2 * LANES]
        column += LANES

    def project(a, carry):
        here = pl.ds(pl.multiple_of(a * size, size), size)
        normed, _ = row_norm(tokens[here, :].astype(f32))
        h = (normed * gains[0:1, :]).astype(bf16)
        normed_low[here, :] = h
        qkv[here, :] = product(h, weights_out[:, : 4 * LANES])
        return carry

    lax.fori_loop(0, blocks, project, 0)

    def prepare(a, carry):
        here = pl.ds(pl.multiple_of(a * size, size), size)
        there = pl.ds(pl.multiple_of((a ^ place[0]) * size, size), size)
        cos_here = jnp.concatenate([cos_part[here, :]] * 4, axis=1)
        sin_here = jnp.concatenate([sin_part[here, :]] * 4, axis=1)
        cosine[here, :], sine[here, :] = cos_here, sin_here

        def turned(x, gain):
            inverse = lax.rsqrt(head_sums(x * x) * (1.0 / HD) + epsilon)
            y = x * inverse * gain
            return y * cos_here + turn(y, 1.0) * sin_here

        for g in range(2):
            q = turned(qkv[there, g * LANES : (g + 1) * LANES], gain_q[...])
            q_out[here, g * LANES : (g + 1) * LANES] = (q.astype(bf16).astype(f32) * score_scale).astype(bf16)
        k = turned(qkv[there, 2 * LANES : 3 * LANES], gain_k[...]).astype(bf16)
        v = qkv[there, 3 * LANES : 4 * LANES].astype(bf16)
        k_out[here, :] = k
        v_out[here, :] = v
        return carry

    lax.fori_loop(0, blocks, prepare, 0)


def attention_kernel(
    place, places, weights, q_in, k_in, v_in, attended, inverse_total, send, keep, keys, values, total,
):
    blocks, size = 4, q_in.shape[0] // 4
    low = lane_ids(size) < HD

    def prepare(a, carry):
        here = pl.ds(pl.multiple_of(a * size, size), size)
        k, v = k_in[here, :].astype(f32), v_in[here, :].astype(f32)
        for h, (one, two) in enumerate(zip(spread_heads(k, 0.0), spread_heads(v, 1.0))):
            keys[h, here, :] = one.astype(bf16)
            values[h, here, :] = two.astype(bf16)
        return carry

    lax.fori_loop(0, blocks, prepare, 0)
    offset = lax.broadcasted_iota(jnp.int32, (size, size), 0) - lax.broadcasted_iota(jnp.int32, (size, size), 1)

    def query_block(i, carry):
        here = pl.ds(pl.multiple_of(i * size, size), size)
        there = pl.ds(pl.multiple_of((i ^ place[0]) * size, size), size)
        total[...] = jnp.zeros_like(total)
        reach_here = jnp.concatenate([jnp.maximum(places[here, :], 0)] * (size // LANES), axis=1)

        def key_block(j, inner):
            at = pl.ds(pl.multiple_of(j * size, size), size)
            distance = offset + (i - j) * size
            allowed = (distance >= 0) & (distance <= reach_here)
            for h in range(4):
                q = q_in[here, (h // 2) * LANES : (h // 2 + 1) * LANES]
                weights = jnp.where(allowed, jnp.exp(contract_cols(q, keys[h, at, :])), 0.0)
                total[h] += product(weights.astype(bf16), values[h, at, :])
            return inner

        lax.fori_loop(0, i + 1, key_block, 0)
        for g in range(2):
            first, second = total[2 * g], total[2 * g + 1]
            inverse = 1.0 / pltpu.roll(jnp.where(low, second, first), HD, 1)
            cols = slice(g * LANES, (g + 1) * LANES)
            attended[there, cols] = (jnp.where(low, first, second) * inverse).astype(bf16)
            inverse_total[here, cols] = inverse
        return carry

    lax.fori_loop(0, blocks, query_block, 0)
    for j, (out, half) in enumerate([(keep, 0), (send, 0), (keep, 1), (send, 1)]):
        rows = slice(j * size, (j + 1) * size)
        out[half * size : (half + 1) * size, :] = contract_cols(attended[rows, :], weights[:, 4 * LANES :]).astype(bf16)


def backward_kernel(
    place, places, weights, q_in, k_in, v_in, attended, inverse_total, near, near_far, mine, far,
    dq_out, dk_out, dv_out, grad_in, keys, values, keys_t, grad_scaled, grad_aug, dq_t, dk_sum, dv_sum,
):
    blocks, size = 4, q_in.shape[0] // 4
    lane = lane_ids(size)
    low = lane < HD
    for j, rows in enumerate((mine, near, far, near_far)):
        grad_in[j * size : (j + 1) * size, :] = product(rows[...], weights[:, 4 * LANES :]).astype(bf16)

    def prepare(a, carry):
        here = pl.ds(pl.multiple_of(a * size, size), size)
        there = pl.ds(pl.multiple_of((a ^ place[0]) * size, size), size)
        k = spread_heads(k_in[here, :].astype(f32), 0.0)
        v = spread_heads(v_in[here, :].astype(f32), 1.0)
        for h in range(4):
            keys[h, here, :] = k[h].astype(bf16)
            keys_t[h, a] = k[h].T.astype(bf16)
            values[h, here, :] = v[h].astype(bf16)
        for g in range(2):
            cols = slice(g * LANES, (g + 1) * LANES)
            upstream = grad_in[there, cols].astype(f32)
            inverse = inverse_total[here, cols]
            delta = head_sums(upstream * attended[there, cols].astype(f32)) * inverse
            scaled = upstream * inverse
            grad_scaled[here, cols] = scaled.astype(bf16)
            moved = -pltpu.roll(delta, HD, 1)
            high = moved.astype(bf16).astype(f32)
            spare = jnp.where(lane % HD == 0, high, jnp.where(lane % HD == 1, moved - high, 0.0))
            grad_aug[2 * g, here, :] = jnp.where(low, scaled, spare).astype(bf16)
            grad_aug[2 * g + 1, here, :] = jnp.where(low, spare, scaled).astype(bf16)
            dq_t[g, a] = jnp.zeros((LANES, size), f32)
        return carry

    lax.fori_loop(0, blocks, prepare, 0)
    offset = lax.broadcasted_iota(jnp.int32, (size, size), 1) - lax.broadcasted_iota(jnp.int32, (size, size), 0)

    def key_block(j, carry):
        at = pl.ds(pl.multiple_of(j * size, size), size)
        dk_sum[...] = jnp.zeros_like(dk_sum)
        dv_sum[...] = jnp.zeros_like(dv_sum)

        def query_block(i, inner):
            here = pl.ds(pl.multiple_of(i * size, size), size)
            distance = offset + (i - j) * size
            allowed = (distance >= 0) & (distance <= jnp.maximum(places[i], 0))
            for g in range(2):
                cols = slice(g * LANES, (g + 1) * LANES)
                q = q_in[here, cols]
                upstream = grad_scaled[here, cols]
                dk_parts, dv_parts, dq_parts = [], [], []
                for h in (2 * g, 2 * g + 1):
                    weights_t = jnp.where(allowed, jnp.exp(contract_cols(keys[h, at, :], q)), 0.0)
                    share_grad = contract_cols(values[h, at, :], grad_aug[h, here, :])
                    score_grad = (weights_t * share_grad).astype(bf16)
                    dv_parts.append(product(weights_t.astype(bf16), upstream))
                    dk_parts.append(product(score_grad, q))
                    dq_parts.append(product(keys_t[h, j], score_grad))
                dq_t[g, i] += dq_parts[0] + dq_parts[1]
                dk_sum[g] += jnp.where(low, dk_parts[0], dk_parts[1])
                dv_sum[g] += jnp.where(low, dv_parts[0], dv_parts[1])
            return inner

        lax.fori_loop(j, blocks, query_block, 0)

        def folded(sums):
            both = [sums[g] + pltpu.roll(sums[g], HD, 1) for g in range(2)]
            return jnp.where(low, both[0], both[1])

        dk_out[at, :] = folded(dk_sum)
        dv_out[at, :] = folded(dv_sum).astype(bf16)
        return carry

    lax.fori_loop(0, blocks, key_block, 0)

    def finish(a, carry):
        here = pl.ds(pl.multiple_of(a * size, size), size)
        for g in range(2):
            dq_out[here, g * LANES : (g + 1) * LANES] = dq_t[g, a].T * score_scale
        return carry

    lax.fori_loop(0, blocks, finish, 0)


def backward_end_kernel(
    ring, place, tokens, weights, normed_low, qkv, cosine, sine, gain_q, gain_k, attended,
    near, near_far, mine, far, ffn_gain, dq, dk, dv,
    grad_weights, top, bottom, send, keep, grad_attn, grad_gain, grad_qkv,
):
    blocks, size = 4, qkv.shape[0] // 4
    grad_gain[...] = jnp.zeros_like(grad_gain)

    def finish(a, carry):
        here = pl.ds(pl.multiple_of(a * size, size), size)
        there = pl.ds(pl.multiple_of((a ^ place[0]) * size, size), size)
        cos_here, sin_here = cosine[here, :], sine[here, :]
        for part in range(3):
            cols = slice(part * LANES, (part + 1) * LANES)
            gain = gain_q[...] if part < 2 else gain_k[...]
            upstream = dq[here, cols] if part < 2 else dk[here, :]
            upstream = upstream * cos_here - turn(upstream * sin_here, 1.0)
            x = qkv[there, cols]
            inverse = lax.rsqrt(head_sums(x * x) * (1.0 / HD) + epsilon)
            normed = x * inverse
            scaled = upstream * gain
            inner_sum = head_sums(scaled * normed) * (1.0 / HD)
            grad_qkv[there, cols] = (inverse * (scaled - normed * inner_sum)).astype(bf16)
            grad_gain[0:1, cols] += jnp.sum(upstream * normed, axis=0, keepdims=True)
        grad_qkv[there, 3 * LANES : 4 * LANES] = dv[here, :]
        return carry

    lax.fori_loop(0, blocks, finish, 0)
    grad_attn[...] = jnp.zeros_like(grad_attn)
    for j, (out, half) in enumerate([(keep, 0), (send, 0), (keep, 1), (send, 1)]):
        here = slice(j * size, (j + 1) * size)
        back = contract_cols(grad_qkv[here, :], weights[:, : 4 * LANES])
        out[half * size : (half + 1) * size, :] = back.astype(bf16)
        normed, _ = row_norm(tokens[here, :].astype(f32))
        grad_attn[...] += jnp.sum(back * normed, axis=0, keepdims=True)
    blocks = tokens.shape[1] // LANES
    extra = grad_weights.shape[0] // blocks - LANES
    for k in range(0, blocks, 2):
        cols = slice(k * LANES, (k + 2) * LANES)
        first = contract_rows(normed_low[:, cols], grad_qkv[...]).astype(bf16)
        second = jnp.zeros((2 * LANES, 2 * LANES), f32)
        for j, rows in enumerate((mine, near, far, near_far)):
            second += contract_rows(rows[:, cols], attended[j * size : (j + 1) * size, :])
        for n in range(2):
            at = (k + n) * (LANES + extra)
            rows = slice(n * LANES, (n + 1) * LANES)
            grad_weights[at : at + LANES, : 4 * LANES] = first[rows]
            grad_weights[at : at + LANES, 4 * LANES :] = second[rows].astype(bf16)
    if not ring:
        top[...] = jnp.zeros_like(top)
        bottom[...] = jnp.zeros_like(bottom)
        return
    heads = [grad_gain[0:1, part * LANES : (part + 1) * LANES] for part in range(3)]
    heads = [jnp.broadcast_to(h, (8, LANES)) for h in (heads[0] + heads[1], heads[2])]
    heads = [h + pltpu.roll(h, HD, 1) for h in heads]
    heads = jnp.where(lane_ids(8) < HD, heads[0], heads[1])[0:1]
    for k in range(blocks):
        cols = slice(k * LANES, (k + 1) * LANES)
        at = k * (LANES + extra) + LANES
        row = lax.broadcasted_iota(jnp.int32, (extra, LANES), 0) == 0
        for n, values in enumerate((grad_attn[:, cols], ffn_gain[:, cols], heads)):
            values = jnp.where(row, jnp.broadcast_to(values, (extra, LANES)), 0.0)
            grad_weights[at : at + extra, n * LANES : (n + 1) * LANES] = values.astype(bf16)
        grad_weights[at : at + extra, 3 * LANES :] = jnp.zeros((extra, 3 * LANES), bf16)
    half = blocks // 2 * (LANES + extra)
    top[...] = grad_weights[half : half + HD, :]
    bottom[...] = grad_weights[half + HD : half + LANES + extra, :]


def pack_kernel(w_query, w_key, w_value, w_out, gains, out):
    wide = w_query.shape[1]
    out[:LANES, :wide] = w_query[...]
    out[:LANES, wide : wide + LANES] = w_key[...]
    out[:LANES, wide + LANES : wide + 2 * LANES] = w_value[...]
    out[:LANES, wide + 2 * LANES :] = w_out[...].astype(f32).T.astype(bf16)
    out[LANES:, :] = gains[...]


def pack_ffn_kernel(w_gate, w_up, w_down, out):
    step = out.shape[1] // 3
    out[:, :step] = w_gate[...]
    out[:, step : 2 * step] = w_up[...]
    out[:, 2 * step :] = w_down[...].astype(f32).T.astype(bf16)


def unpack_ffn_kernel(mine, up, down, gate, up_out, down_out):
    step = gate.shape[1]

    def total(part):
        cols = slice(part * step, (part + 1) * step)
        return mine[:, cols].astype(f32) + up[:, cols].astype(f32) + down[:, cols].astype(f32)

    gate[...] = total(0)
    up_out[...] = total(1)
    down_out[...] = total(2).T


def unpack_kernel(mine, up, down, query, key, value, out, gains):
    wide = query.shape[1]
    total = mine[:LANES, :].astype(f32) + up[:LANES, :].astype(f32) + down[:LANES, :].astype(f32)
    rest = slice(LANES, LANES + 16)
    gains[...] = (mine[rest, :].astype(f32) + up[rest, :].astype(f32) + down[rest, :].astype(f32))[:8, : 3 * LANES]
    query[...] = total[:, :wide]
    key[...] = total[:, wide : wide + LANES]
    value[...] = total[:, wide + LANES : wide + 2 * LANES]
    out[...] = total[:, wide + 2 * LANES :].T


def arrange_kernel(ring, place, tokens, out):
    for k in range(tokens.shape[1] // LANES):
        out[:, k * LANES : (k + 1) * LANES] = tokens[:, pl.ds(column(place, k, ring), LANES)]


def arrange_live_kernel(ring, place, cotangent, places, out, turned):
    live = places[...] >= 0
    for k in range(cotangent.shape[1] // LANES):
        values = cotangent[:, pl.ds(column(place, k, ring), LANES)].astype(f32)
        values = jnp.where(live, values, 0.0)
        out[:, k * LANES : (k + 1) * LANES] = values.astype(bf16)
        turned[k * LANES : (k + 1) * LANES, :] = values.T.astype(bf16)


def residual_kernel(part, other, far, tokens, gains, residual, low):
    total = part[...].astype(f32) + other[...].astype(f32) + far[...].astype(f32)
    total = tokens[...].astype(f32) + total
    residual[...] = total
    normed, _ = row_norm(total)
    low[...] = (normed * gains[1:2, :]).astype(bf16)


def put_columns(ring, place, out, values):
    for k in range(values.shape[1] // LANES):
        out[:, pl.ds(column(place, k, ring), LANES)] = values[:, k * LANES : (k + 1) * LANES].astype(out.dtype)


def norm_back(upstream, gain, normed, inverse):
    scaled = upstream * gain
    inner_sum = jnp.mean(scaled * normed, axis=-1, keepdims=True)
    return inverse * (scaled - normed * inner_sum)


def residual_back_kernel(part, other, far, residual, gains, output_low, grad, low, gain_out):
    upstream = part[...].astype(f32) + other[...].astype(f32) + far[...].astype(f32)
    normed, inverse = row_norm(residual[...])
    total = output_low[...].astype(f32) + norm_back(upstream, gains[1:2, :], normed, inverse)
    grad[...] = total
    low[...] = total.astype(bf16)
    gain_out[...] = jnp.sum(upstream * normed, axis=0, keepdims=True)


def output_kernel(ring, place, part, other, far, residual, out):
    total = part[...].astype(f32) + other[...].astype(f32) + far[...].astype(f32)
    put_columns(ring, place, out, residual[...] + total)


def input_back_kernel(ring, place, part, other, far, tokens, gains, grad, out):
    upstream = part[...].astype(f32) + other[...].astype(f32) + far[...].astype(f32)
    normed, inverse = row_norm(tokens[...].astype(f32))
    put_columns(ring, place, out, grad[...] + norm_back(upstream, gains[0:1, :], normed, inverse))


def ffn_kernel(near, near_far, mine, far, output_low, output_t, *refs):
    pieces, rest = refs[:9], refs[9:]
    low_t, active, out_send, out_keep, in_send, in_keep, first_grad, top, bottom, weights, low, low_pair = rest
    size = mine.shape[0]
    step = weights.shape[1] // 3
    half = pl.program_id(0)

    @pl.when(half == 0)
    def _():
        assemble(pieces, weights)
        low[:size, :] = near[...]
        low[size:, :] = near_far[...]

    @pl.when(half == 1)
    def _():
        low[:size, :] = mine[...]
        low[size:, :] = far[...]

    low_t[...] = low[...].T
    here = pl.ds(pl.multiple_of(half * 2 * size, 2 * size), 2 * size)
    pair = slice(weights.shape[0] // 2, weights.shape[0] // 2 + 2 * LANES)
    for first in range(0, step, 256):
        last = min(first + 256, step)
        gate = product(low[...], weights[:, first:last])
        up = product(low[...], weights[:, step + first : step + last])
        hidden_grad = product(output_low[...], weights[:, 2 * step + first : 2 * step + last])
        sigmoid = 0.5 + 0.5 * jnp.tanh(0.5 * gate)
        silu = gate * sigmoid
        active[here, 2 * step + first : 2 * step + last] = (silu * up).astype(bf16)
        active[here, first:last] = (hidden_grad * up * (sigmoid + silu * (1.0 - sigmoid))).astype(bf16)
        active[here, step + first : step + last] = (hidden_grad * silu).astype(bf16)
    out = contract_cols(active[here, 2 * step :], weights[:, 2 * step :])
    into = contract_cols(active[here, : 2 * step], weights[:, : 2 * step])

    @pl.when(half == 0)
    def _():
        out_send[...] = out.astype(bf16)
        in_send[...] = into.astype(bf16)
        low_pair[:, : 2 * size] = low_t[pair, :]

    @pl.when(half == 1)
    def _():
        out_keep[...] = out.astype(bf16)
        in_keep[...] = into.astype(bf16)
        low_pair[:, 2 * size :] = low_t[pair, :]
        first_grad[:, : 2 * step] = product(low_pair[...], active[:, : 2 * step]).astype(bf16)
        first_grad[:, 2 * step :] = product(output_t[...], active[:, 2 * step :]).astype(bf16)
        top[...] = first_grad[:HD, :]
        bottom[...] = first_grad[HD:LANES, :]


def ffn_weights_kernel(low_t, output_t, active, out, top, bottom):
    step = active.shape[1] // 3
    out[:, : 2 * step] = product(low_t[...], active[:, : 2 * step]).astype(bf16)
    out[:, 2 * step :] = product(output_t[...], active[:, 2 * step :]).astype(bf16)

    @pl.when(pl.program_id(0) == 0)
    def _():
        top[...] = out[:HD, :]
        bottom[...] = out[HD:LANES, :]


def shape_of(*dims, dtype=bf16):
    return jax.ShapeDtypeStruct(dims, dtype)


def params(mebibytes=48):
    return pltpu.CompilerParams(vmem_limit_bytes=mebibytes * 2**20)


def cost(flops, bytes_moved, exps=0, share=1.0):
    return pl.CostEstimate(flops=int(share * flops), bytes_accessed=int(share * bytes_moved), transcendentals=int(share * exps))


def simple(kernel, outs, name, args, n_scalars=0):
    return pl.pallas_call(
        kernel,
        out_shape=outs,
        in_specs=[scalars] * n_scalars + [whole_vmem] * (len(args) - n_scalars),
        out_specs=jax.tree.map(lambda _: whole_vmem, outs),
        compiler_params=params(),
        name=name,
    )(*args)


def first_rows(rows, cols, at=0):
    return pl.BlockSpec((rows, cols), lambda i: (at, 0))


def own_rows(kernel, rows, width, outs, name, place, args, places=()):
    specs = [scalars] if place is not None else []
    specs += [first_rows(min(rows, a.shape[0]), width, dict(places).get(n, 0)) for n, a in enumerate(args)]
    return pl.pallas_call(
        kernel,
        grid=(1,),
        out_shape=outs,
        in_specs=specs,
        out_specs=tuple(first_rows(o.shape[0], width) for o in outs),
        compiler_params=params(),
        cost_estimate=cost(8 * rows * width, 12 * rows * width),
        name=name,
    )(*([place] if place is not None else []), *args)


def feed_forward(rows_in, output_low, output_t, pieces):
    slots, width = output_low.shape
    cols = pieces[0].shape[1]
    half = slots // 2
    wide = shape_of(half, width)
    moving = lambda n: pl.BlockSpec((half, n), lambda i: (i, 0))
    return pl.pallas_call(
        ffn_kernel,
        grid=(2,),
        out_shape=(shape_of(width, slots), shape_of(slots, cols), wide, wide, wide, wide)
        + (shape_of(2 * LANES, cols), shape_of(HD, cols), shape_of(HD, cols)),
        in_specs=[whole_vmem] * 4
        + [moving(width), pl.BlockSpec((2 * LANES, slots), lambda i: (width // (4 * LANES), 0))]
        + [whole_vmem] * 9,
        out_specs=(pl.BlockSpec((width, half), lambda i: (0, i)), whole_vmem) + (whole_vmem,) * 7,
        scratch_shapes=[pltpu.VMEM((width, cols), bf16), pltpu.VMEM((half, width), bf16), pltpu.VMEM((2 * LANES, slots), bf16)],
        compiler_params=params(56),
        cost_estimate=cost(4 * slots * width * cols, 20 * 2**20, 2e6),
        name="ffn",
    )(*rows_in, output_low, output_t, *pieces)


def feed_forward_weights(low_t, output_t, active, first, number):
    width, slots = low_t.shape
    cols = active.shape[1]
    pair = 2 * LANES
    pairs = width // pair
    side = pl.BlockSpec((pair, slots), lambda i: (lax.rem(i + first, pairs), 0))
    return pl.pallas_call(
        ffn_weights_kernel,
        grid=(number,),
        out_shape=(shape_of(number * pair, cols), shape_of(HD, cols), shape_of(HD, cols)),
        in_specs=[side, side, whole_vmem],
        out_specs=(pl.BlockSpec((pair, cols), lambda i: (i, 0)), whole_vmem, whole_vmem),
        compiler_params=params(),
        cost_estimate=cost(2 * slots * pair * number * cols, 12 * 2**20),
        name="ffn_weights",
    )(low_t, output_t, active)


def rotary_tables(slot_positions):
    powers = jnp.arange(HD // 2, dtype=f32) * (2.0 / HD)
    frequency = rope_base ** (-powers)
    angles = jnp.maximum(slot_positions, 0).astype(f32)[:, None] * frequency[None, :]
    return jnp.cos(angles), jnp.sin(angles)


def per_device(
    tokens, positions, attn_gain, query_gain, key_gain, w_query, w_key, w_value, w_out, ffn_gain,
    w_gate, w_up, w_down, cotangent,
):
    slots, width = tokens.shape
    count = lax.axis_size("dp")
    me = lax.axis_index("dp")
    place = lax.axis_index("tensor").astype(jnp.int32)
    rows = slots // 4
    ring = count * LANES == width and count % 2 == 0
    hidden = w_gate.shape[1]
    q_cols, k_cols = w_query.shape[1], w_key.shape[1]
    attn_cols = q_cols + 2 * k_cols + w_out.shape[0]

    if ring:
        spot = jnp.where(me % 2 == 0, me // 2, count - 1 - me // 2)
    else:
        spot = me
    length = count if ring else 0
    place = jnp.stack([place, spot.astype(jnp.int32)])

    def in_place(kernel):
        return functools.partial(kernel, length)

    if ring:
        gains_row = jnp.pad(
            jnp.concatenate([attn_gain, ffn_gain])[None, :], ((0, 15), (0, attn_cols - 2 * LANES))
        )
        shards = (w_query, w_key, w_value, w_out, gains_row)
        attn_block = pl.pallas_call(
            pack_kernel,
            grid=(1,),
            out_shape=shape_of(LANES + 16, attn_cols),
            in_specs=[first_rows(*a.shape) for a in shards],
            out_specs=first_rows(LANES + 16, attn_cols),
            name="pack",
        )(*shards)
        ffn_block = simple(pack_ffn_kernel, shape_of(LANES, 3 * hidden), "pack_ffn", (w_gate, w_up, w_down))
    else:
        gathered = lax.all_gather(
            jnp.concatenate([w_query, w_key, w_value, w_out.T], axis=1), "dp", axis=0, tiled=True
        )
        gains_all = jnp.stack(
            [lax.all_gather(g, "dp", axis=0, tiled=True) for g in (attn_gain, ffn_gain)], axis=0
        )
        attn_pieces = []
        for k, piece in enumerate(pieces_of(gathered)):
            column = k * LANES if k < 4 else (k - 1) * LANES
            pad = jnp.pad(
                gains_all[:, column : column + LANES].reshape(1, -1), ((0, 15), (0, attn_cols - 2 * LANES))
            )
            attn_pieces.append(piece if k == 4 else jnp.concatenate([piece, pad], axis=0))
        turned = w_down.T
        block = lax.all_gather(jnp.concatenate([w_gate, w_up, turned], axis=1), "dp", axis=0, tiled=True)
        ffn_pieces = pieces_of(block)

    places = jnp.broadcast_to(positions[:, None], (slots, LANES))
    place_rows = positions.reshape(4, 1, rows)
    straight = pl.BlockSpec((rows, width), lambda i, s: (i, 0))

    def arranged(kernel, row_of, args, name, turned=False):
        return pl.pallas_call(
            in_place(kernel),
            out_shape=(shape_of(slots, width), shape_of(width, slots)) if turned else shape_of(slots, width),
            grid_spec=pltpu.PrefetchScalarGridSpec(
                num_scalar_prefetch=1,
                grid=(4,),
                in_specs=[pl.BlockSpec((rows, a.shape[1]), lambda i, s: (row_of(i) ^ s[0], 0)) for a in args],
                out_specs=(straight, pl.BlockSpec((width, rows), lambda i, s: (0, i))) if turned else straight,
            ),
            cost_estimate=cost(0, 4 * slots * width),
            name=name,
        )(place, *args)

    inputs = arranged(arrange_kernel, lambda i: i, (tokens,), "arrange")
    output_low, output_t = arranged(
        arrange_live_kernel, lambda i: lax.rem(2 * i + 1, 5), (cotangent, places), "arrange_live", True
    )
    tables = rotary_tables(positions)
    if ring:
        attn_ring, ffn_ring = RingGather(attn_block, count), RingGather(ffn_block, count)
        attn_ring.send()
        attn_ring.tie(ffn_block)
        attn_ring.send()
        (inputs,) = attn_ring.tie(inputs)
        attn_ring.send()
        tables = attn_ring.tie(*tables)
        attn_ring.send()
        ffn_ring.moving = after(ffn_ring.moving, attn_ring.moving)
        ffn_ring.send()
        attn_pieces = attn_ring.pieces()
    gain_q = jnp.tile(query_gain.astype(f32), 2)[None, :]
    gain_k = jnp.tile(key_gain.astype(f32), 2)[None, :]

    weights, gains, normed_low, qkv, q, k, v, cosine, sine = pl.pallas_call(
        project_kernel,
        out_shape=(
            shape_of(width, attn_cols),
            shape_of(8, width, dtype=f32),
            shape_of(slots, width),
            shape_of(slots, 4 * LANES, dtype=f32),
            shape_of(slots, 2 * LANES),
            shape_of(slots, LANES),
            shape_of(slots, LANES),
            shape_of(slots, LANES, dtype=f32),
            shape_of(slots, LANES, dtype=f32),
        ),
        in_specs=[scalars] + [whole_vmem] * 14,
        out_specs=(whole_vmem,) * 9,
        compiler_params=params(),
        cost_estimate=cost(3e9, 14 * 2**20, 3e6),
        name="project",
    )(place, inputs, *tables, gain_q, gain_k, *attn_pieces)
    halved = shape_of(slots // 2, width)
    attended, inverse_total, attn_send, attn_keep = pl.pallas_call(
        attention_kernel,
        out_shape=(shape_of(slots, 2 * LANES), shape_of(slots, 2 * LANES, dtype=f32), halved, halved),
        in_specs=[scalars] + [whole_vmem] * 5,
        out_specs=(whole_vmem,) * 4,
        scratch_shapes=[
            pltpu.VMEM((4, slots, LANES), bf16),
            pltpu.VMEM((4, slots, LANES), bf16),
            pltpu.VMEM((4, rows, LANES), f32),
        ],
        compiler_params=params(),
        cost_estimate=cost(9e9, 8 * 2**20, 3e6),
        name="attention",
    )(place, places, weights, q, k, v)

    other = swap(attn_send, "tensor", 1)
    if ring:
        (other,) = after((other,), ffn_ring.moving)
        ffn_ring.send()
    far = swap(add(attn_keep[rows:], other[rows:]), "tensor", 2)
    if ring:
        (far,) = after((far,), ffn_ring.moving)
        ffn_ring.send()
    row_f32, row_bf16 = shape_of(rows, width, dtype=f32), shape_of(rows, width)
    one_gain = shape_of(1, width, dtype=f32)
    residual, ffn_rows = own_rows(
        residual_kernel, rows, width, (row_f32, row_bf16), "residual", None, (attn_keep, other, far, inputs, gains)
    )
    near, far = swap(ffn_rows, "tensor", 1), swap(ffn_rows, "tensor", 2)
    if ring:
        ffn_ring.send()
        ffn_pieces = ffn_ring.pieces()
    rows_in = near, swap(far, "tensor", 1), ffn_rows, far

    ffn_low_t, active, out_send, out_keep, in_send, in_keep, first_grad, top, bottom = feed_forward(
        rows_in, output_low, output_t, ffn_pieces
    )
    other = swap(in_send, "tensor", 1)
    if ring:
        half = count // 2
        toward_y = add(in_keep[rows:], other[rows:])
        (active,) = after((active,), (toward_y,))
        next_grad, _, _ = feed_forward_weights(ffn_low_t, output_t, active, half // 2 - 1, 1)
        ffn_grads = {half // 2: first_grad, half // 2 - 1: next_grad}

        def ffn_block_of(k):
            return ffn_grads[k // 2][k % 2 * LANES : (k % 2 + 1) * LANES]

        ffn_scatter = RingScatter(ffn_block_of, top, bottom, count)
        ffn_scatter.send()
        far = swap(toward_y, "tensor", 2)
    else:
        grad_ffn, _, _ = feed_forward_weights(ffn_low_t, output_t, active, 0, width // (2 * LANES))
        far = swap(add(in_keep[rows:], other[rows:]), "tensor", 2)
    residual_grad, residual_low, ffn_gain_part = own_rows(
        residual_back_kernel, rows, width, (row_f32, row_bf16, one_gain), "residual_back", None,
        (in_keep, other, far, residual, gains, output_low), [(5, 2)],
    )
    near, far = swap(residual_low, "tensor", 1), swap(residual_low, "tensor", 2)
    out_other = swap(out_send, "tensor", 1)
    out_toward_y = add(out_keep[rows:], out_other[rows:])
    if ring:
        (far,), (out_toward_y,) = tied((far,), (out_toward_y,))
    out_far = swap(out_toward_y, "tensor", 2)
    rows_back = near, swap(far, "tensor", 1), residual_low, far
    if ring:
        (active,) = after((active,), (residual_low,))
        ffn_scatter.moving = after(ffn_scatter.moving, (residual_low,))
        ffn_scatter.add()
        ffn_scatter.send()
        rest_grad, _, _ = feed_forward_weights(ffn_low_t, output_t, active, half // 2 + 1, half // 2)
        ffn_grads[half // 2 + 1], ffn_grads[0] = rest_grad[: 2 * LANES], rest_grad[2 * LANES :]
        ffn_scatter.add()
        rows_back = after(rows_back, (*ffn_scatter.moving, out_far))
        ffn_scatter.send()

    grads = pl.pallas_call(
        backward_kernel,
        out_shape=(
            shape_of(slots, 2 * LANES, dtype=f32), shape_of(slots, LANES, dtype=f32), shape_of(slots, LANES),
        ),
        in_specs=[scalars] + [whole_vmem] * 11,
        out_specs=(whole_vmem,) * 3,
        scratch_shapes=[
            pltpu.VMEM((slots, 2 * LANES), bf16),
            pltpu.VMEM((4, slots, LANES), bf16),
            pltpu.VMEM((4, slots, LANES), bf16),
            pltpu.VMEM((4, 4, LANES, rows), bf16),
            pltpu.VMEM((slots, 2 * LANES), bf16),
            pltpu.VMEM((4, slots, LANES), bf16),
            pltpu.VMEM((2, 4, LANES, rows), f32),
            pltpu.VMEM((2, rows, LANES), f32),
            pltpu.VMEM((2, rows, LANES), f32),
        ],
        compiler_params=params(),
        cost_estimate=cost(16e9, 8 * 2**20, 3e6),
        name="attention_backward",
    )(place, place_rows, weights, q, k, v, attended, inverse_total, *rows_back)
    if ring:
        ffn_scatter.add()
        grads = after(grads, ffn_scatter.moving)
        ffn_scatter.send()
    tall = LANES + 16 if ring else LANES
    grad_attn, top, bottom, attn_send, attn_keep, attn_gain_part, head_gains = pl.pallas_call(
        in_place(backward_end_kernel),
        out_shape=(
            shape_of(width // LANES * tall, attn_cols),
            shape_of(HD, attn_cols),
            shape_of(tall - HD, attn_cols),
            halved,
            halved,
            one_gain,
            shape_of(8, 3 * LANES, dtype=f32),
        ),
        in_specs=[scalars] + [whole_vmem] * 17,
        out_specs=(whole_vmem,) * 7,
        scratch_shapes=[pltpu.VMEM((slots, 4 * LANES), bf16)],
        compiler_params=params(),
        cost_estimate=cost(9e9, 14 * 2**20),
        name="backward_end",
    )(
        place, inputs, weights, normed_low, qkv, cosine, sine, gain_q, gain_k, attended, *rows_back,
        ffn_gain_part, *grads,
    )

    (block_output,) = own_rows(
        in_place(output_kernel), rows, width, (row_bf16,), "output", place, (out_keep, out_other, out_far, residual)
    )
    other, far = tensor_scatter(attn_send, attn_keep)
    (input_grad,) = own_rows(
        in_place(input_back_kernel), rows, width, (row_bf16,), "input_back", place,
        (attn_keep, other, far, inputs, gains, residual_grad),
    )
    if ring:
        attn_scatter = RingScatter(lambda k: grad_attn[k * tall : (k + 1) * tall], top, bottom, count)
        attn_scatter.send()
        shard_gate, shard_up, shard_down = simple(
            unpack_ffn_kernel,
            tuple(jax.ShapeDtypeStruct(w.shape, f32) for w in (w_gate, w_up, w_down)),
            "unpack_ffn",
            (ffn_block_of(0), *ffn_scatter.moving),
        )
        for step in range(half - 1):
            attn_scatter.add()
            if step == 0:
                attn_scatter.moving = after(attn_scatter.moving, ffn_scatter.moving)
            if step == half - 2:
                attn_scatter.moving = after(attn_scatter.moving, (far, shard_gate, block_output))
            attn_scatter.send()
        shard_query, shard_key, shard_value, shard_out, gain_part = simple(
            unpack_kernel,
            (*(shape_of(*w.shape, dtype=f32) for w in (w_query, w_key, w_value, w_out)), shape_of(8, 3 * LANES, dtype=f32)),
            "unpack",
            (grad_attn[:tall], *attn_scatter.moving),
        )
        gain_total = gain_part + sum(swap(gain_part, "tensor", bits) for bits in (1, 2, 3))
        grad_attn_gain, grad_ffn_gain, heads = (gain_total[0, k * LANES : (k + 1) * LANES] for k in range(3))
        grad_query_gain, grad_key_gain = heads[:HD], heads[HD:]
    else:
        gain_total = sum_all(jnp.concatenate([attn_gain_part, ffn_gain_part, head_gains[0:1]], axis=1))[0]
        share = width // count
        grad_attn_gain = lax.dynamic_slice_in_dim(gain_total, me * share, share)
        grad_ffn_gain = lax.dynamic_slice_in_dim(gain_total, width + me * share, share)
        heads = gain_total[2 * width :].reshape(-1, HD)
        grad_query_gain = jnp.sum(heads[:4], axis=0)
        grad_key_gain = jnp.sum(heads[4:], axis=0)
        total = lax.psum_scatter(grad_attn, "dp", scatter_dimension=0, tiled=True).astype(f32)
        shard_query, shard_key, shard_value, turned = jnp.split(total, np.cumsum([q_cols, k_cols, k_cols]), axis=1)
        shard_out = turned.T
        total = lax.psum_scatter(grad_ffn, "dp", scatter_dimension=0, tiled=True).astype(f32)
        shard_gate, shard_up, turned = jnp.split(total, 3, axis=1)
        shard_down = turned.T
    return (
        block_output,
        input_grad,
        grad_attn_gain,
        grad_query_gain,
        grad_key_gain,
        shard_query,
        shard_key,
        shard_value,
        shard_out,
        grad_ffn_gain,
        shard_gate,
        shard_up,
        shard_down,
    )


def solution(mesh):
    in_specs = (
        P("dp", None), P("dp"), P("dp"), P(), P(), P("dp", "tensor"), P("dp", "tensor"), P("dp", "tensor"),
        P("tensor", "dp"), P("dp"), P("dp", "tensor"), P("dp", "tensor"), P("tensor", "dp"), P("dp", None),
    )
    out_specs = (
        P(("dp", "tensor"), None), P(("dp", "tensor"), None), P("dp"), P(), P(), P("dp", "tensor"),
        P("dp", "tensor"), P("dp", "tensor"), P("tensor", "dp"), P("dp"), P("dp", "tensor"), P("dp", "tensor"),
        P("tensor", "dp"),
    )
    return jax.shard_map(
        per_device, mesh=mesh, in_specs=in_specs, out_specs=out_specs, check_vma=False
    )
```
